256 devices in a mesh: gx: 2 (over core), gy: 64 (over z, y, x_hi), rep: 2 (over x_lo).
Axes of the slice: x: 4 (x_hi: 2, x_lo: 2; x = x_hi * 2 + x_lo), y: 4, z: 8, core: 2. Of those that a mesh axis runs over, the one named last changes fastest.
Arguments:
- feats: bfloat16 [262144, 256], P(('gx', 'gy', 'rep')), may hold values from -6 to 6
- weight: bfloat16 [27, 256, 256], P(None, None, 'rep'), may hold values from -0.109375 to 0.109375
- cotan: bfloat16 [262144, 256], P(('gx', 'gy', 'rep')), may hold values from -24 to 24
- face_send: int32 [256, 4, 4], P(('gx', 'gy', 'rep')), may hold values from 0 to 7
- corner_send: int32 [256, 4, 1], P(('gx', 'gy', 'rep')), may hold values from 0 to 7
- pair_out: int32 [256, 27, 4], P(('gx', 'gy', 'rep')), may hold values from 0 to 7
- pair_in: int32 [256, 27, 4], P(('gx', 'gy', 'rep')), may hold values from 0 to 28
- row_map: int32 [256, 27, 4, 128], P(('gx', 'gy', 'rep')), may hold values from 0 to 128
Outputs:
- activation: bfloat16 [262144, 256], P(('gx', 'gy', 'rep'))
- input_grad: bfloat16 [262144, 256], P(('gx', 'gy', 'rep'))
- weight_grad: float32 [27, 256, 256], P(None, None, 'rep')
The draws below stay inside these ranges and needn't reach their ends.
All inputs are finite; a program needn't handle non-finite values.
Results may differ from the reference program's by a relative error of at most 0.007.
Values may be sent and summed in bfloat16 or wider, within the bound.
No kernel may reach another device: no remote copies, remote signals or barrier semaphores. Data moves between devices by JAX's collectives and lax.ppermute only.
A program may use at most 128 MiB of HBM per device.

```python
import jax
import jax.numpy as jnp
from jax import lax

C = 256
K = 27
NB = 8
HF = 4
HC = 1
P_SIZE = 4
EXT_BLOCKS = 28
TILES = 256
VOXELS = 262144
N_GX = 2
N_GY = 64
N_REP = 2


def plant(array, key, smallest, high):
    index_at = [jax.random.randint(jax.random.fold_in(key, axis), (), 0, length) for axis, length in enumerate(array.shape)]
    widest = array.shape.index(max(array.shape))
    next_to = index_at[:widest] + [(index_at[widest] + 1) % array.shape[widest]] + index_at[widest + 1:]
    return array.at[tuple(index_at)].set(smallest).at[tuple(next_to)].set(high)


def with_spikes(drawn, key, source, target, parts, factor):
    owner, partner = [(jnp.arange(drawn.shape[position]) // (drawn.shape[position] // parts)).reshape([-1 if axis == position else 1 for axis in range(drawn.ndim)]) for position in (source, target)]
    chosen = jax.random.permutation(key, parts)[partner]
    strong = (owner == chosen) | (owner == (partner + parts // 2) % parts)
    return jnp.where(strong, factor * drawn, drawn)


def level_of(rng, extent, split, low, largest):
    level = 1.0
    for position, parts in split:
        steps = jax.random.uniform(jax.random.fold_in(jax.random.fold_in(rng, 6), position), (parts,), jnp.float32, low / len(split), largest / len(split))
        level = level * jnp.repeat(jnp.exp(steps), extent[position] // parts).reshape((-1,) + (1,) * (len(extent) - 1 - position))
    return level


def scatter_about(key, dims, scale, most, shards=(), kind=jnp.bfloat16):
    drawn = scale * jax.random.normal(key, dims, jnp.float32)
    if shards:
        drawn = drawn * level_of(key, dims, shards, -0.22, 0.18)
    return jnp.clip(drawn, -most, most).astype(kind)


def noise_with(key, extent, spread, reach, cuts, heavy, kind=jnp.bfloat16):
    drawn = spread * jax.random.normal(key, extent, jnp.float32)
    if cuts:
        drawn = drawn * level_of(key, extent, cuts, -0.22, 0.18)
    return jnp.clip(with_spikes(drawn, jax.random.fold_in(key, 3), *heavy), -reach, reach).astype(kind)


def setup_inputs(seed: int = 0) -> dict:
    keys = jax.random.split(jax.random.key(seed), 9)
    feats = scatter_about(keys[0], (VOXELS, C), 1.0, 6.0, ((0, 256),))
    weight = scatter_about(keys[1], (K, C, C), (K * P_SIZE * C // NB) ** -0.5, 0.109375, ((2, 2),))
    cotan = noise_with(keys[2], (VOXELS, C), 1.0, 24.0, ((0, 256),), (0, 1, 256, 6.0))
    face_send = plant(jax.random.randint(keys[3], (TILES, 4, HF), 0, NB), jax.random.fold_in(keys[3], 1), 0, NB - 1).astype(jnp.int32)
    corner_send = plant(jax.random.randint(keys[4], (TILES, 4, HC), 0, NB), jax.random.fold_in(keys[4], 1), 0, NB - 1).astype(jnp.int32)
    pair_out = plant(jax.random.randint(keys[5], (TILES, K, P_SIZE), 0, NB), jax.random.fold_in(keys[5], 1), 0, NB - 1).astype(jnp.int32)
    pair_in = plant(jax.random.randint(keys[6], (TILES, K, P_SIZE), 0, EXT_BLOCKS + 1), jax.random.fold_in(keys[6], 1), 0, EXT_BLOCKS).astype(jnp.int32)
    row_map = plant(jax.random.randint(keys[7], (TILES, K, P_SIZE, 128), 0, 129), jax.random.fold_in(keys[7], 1), 0, 128).astype(jnp.int32)
    return dict(feats=feats, weight=weight, cotan=cotan, face_send=face_send, corner_send=corner_send, pair_out=pair_out, pair_in=pair_in, row_map=row_map)


face_steps = ((-1, 0), (1, 0), (0, -1), (0, 1))
face_back = (1, 0, 3, 2)
corner_steps = ((-1, -1), (-1, 1), (1, -1), (1, 1))

def silu_grad(values):
    sigma = jax.nn.sigmoid(values)
    return sigma * (1.0 + values * (1.0 - sigma))

def gather_rows(flat_rows, ins_k, map_k, zero_row):
    source = ins_k[:, None] * 128 + map_k
    source = jnp.where(map_k == 128, zero_row, source).astype(jnp.int32)
    return (flat_rows[source], source)

def flatten_ext(ext_blocks):
    channels = ext_blocks.shape[2]
    flat_rows = jnp.concatenate([ext_blocks.reshape(-1, channels), jnp.zeros((1, channels), ext_blocks.dtype)], 0)
    return (flat_rows, ext_blocks.shape[0] * 128)

def forward_local(ext_blocks, weight, outs_all, ins_all, maps_all, block_count):
    channels = ext_blocks.shape[2]
    flat_rows, zero_row = flatten_ext(ext_blocks)
    block_ids = jnp.arange(block_count, dtype=jnp.int32)

    def one_offset(running, packed):
        weight_k, outs_k, ins_k, map_k = packed
        rows_k, source = gather_rows(flat_rows, ins_k, map_k, zero_row)
        pieces_count = rows_k.shape[0]
        product = jnp.dot(rows_k.reshape(-1, channels), weight_k, preferred_element_type=jnp.float32)
        product = product.reshape(pieces_count, 128, channels)
        select = (outs_k[None, :] == block_ids[:, None]).astype(jnp.float32)
        added = jnp.einsum('bp,prc->brc', select, product, precision=lax.Precision.HIGHEST)
        return (running + added, None)
    start_sum = jnp.zeros((block_count, 128, channels), jnp.float32)
    pre_act, unused_out = lax.scan(one_offset, start_sum, (weight, outs_all, ins_all, maps_all))
    return pre_act

def backward_local(ext_blocks, weight, outs_all, ins_all, maps_all, pre_grad):
    channels = ext_blocks.shape[2]
    flat_rows, zero_row = flatten_ext(ext_blocks)

    def one_offset(grad_rows, packed):
        weight_k, outs_k, ins_k, map_k = packed
        rows_k, source = gather_rows(flat_rows, ins_k, map_k, zero_row)
        upstream = pre_grad[outs_k]
        flat_up = upstream.reshape(-1, channels)
        back_rows = lax.dot_general(flat_up, weight_k, (((1,), (1,)), ((), ())), preferred_element_type=jnp.float32)
        grad_rows = grad_rows.at[source.reshape(-1)].add(back_rows)
        weight_piece = lax.dot_general(rows_k.reshape(-1, channels), flat_up, (((0,), (0,)), ((), ())), preferred_element_type=jnp.float32)
        return (grad_rows, weight_piece)
    start_rows = jnp.zeros((zero_row + 1, channels), jnp.float32)
    grad_rows, weight_part = lax.scan(one_offset, start_rows, (weight, outs_all, ins_all, maps_all))
    ext_grad = grad_rows[:zero_row].reshape(-1, 128, channels)
    return (ext_grad, weight_part)

def reference(feats, weight, cotan, face_send, corner_send, pair_out, pair_in, row_map):
    channels = feats.shape[1]
    tile_blocks = feats.reshape(N_GX, N_GY, N_REP, NB, 128, channels)
    face_lists = face_send.reshape(N_GX, N_GY, N_REP, 4, HF)
    corner_lists = corner_send.reshape(N_GX, N_GY, N_REP, 4, HC)
    cot_blocks = cotan.reshape(TILES, NB, 128, channels)
    tile_ids = jnp.arange(TILES, dtype=jnp.int32)

    def locate(tile_id):
        return (tile_id // (N_GY * N_REP), tile_id // N_REP % N_GY, tile_id % N_REP)

    def neighbour(pos_x, pos_y, step_x, step_y):
        near_x = pos_x + step_x
        near_y = pos_y + step_y
        inside = (near_x >= 0) & (near_x < N_GX) & (near_y >= 0) & (near_y < N_GY)
        return (jnp.clip(near_x, 0, N_GX - 1), jnp.clip(near_y, 0, N_GY - 1), inside)

    def build_ext(tile_id):
        pos_x, pos_y, replica = locate(tile_id)
        pieces = [tile_blocks[pos_x, pos_y, replica]]
        for slot_id, (step_x, step_y) in enumerate(face_steps):
            near_x, near_y, inside = neighbour(pos_x, pos_y, step_x, step_y)
            listed = face_lists[near_x, near_y, replica, face_back[slot_id]]
            moved_blocks = tile_blocks[near_x, near_y, replica][listed]
            pieces.append(jnp.where(inside, moved_blocks, jnp.zeros_like(moved_blocks)))
        for slot_id, (step_x, step_y) in enumerate(corner_steps):
            near_x, near_y, inside = neighbour(pos_x, pos_y, step_x, step_y)
            listed = corner_lists[near_x, near_y, replica, 3 - slot_id]
            moved_blocks = tile_blocks[near_x, near_y, replica][listed]
            pieces.append(jnp.where(inside, moved_blocks, jnp.zeros_like(moved_blocks)))
        pieces.append(jnp.zeros((1, 128, channels), feats.dtype))
        return jnp.concatenate(pieces, 0)

    def first_pass(running, tile_id):
        ext_blocks = build_ext(tile_id)
        pre_act = forward_local(ext_blocks, weight, pair_out[tile_id], pair_in[tile_id], row_map[tile_id], NB)
        activation = jax.nn.silu(pre_act).astype(jnp.bfloat16)
        pre_grad = (cot_blocks[tile_id].astype(jnp.float32) * silu_grad(pre_act)).astype(jnp.bfloat16)
        ext_grad, weight_part = backward_local(ext_blocks, weight, pair_out[tile_id], pair_in[tile_id], row_map[tile_id], pre_grad)
        rounded = lax.optimization_barrier(weight_part.astype(jnp.bfloat16))
        running = running + rounded.astype(jnp.float32)
        halo_grad = ext_grad[NB:EXT_BLOCKS].astype(jnp.bfloat16)
        return (running, (activation, ext_grad[:NB], halo_grad))
    start_grad = jnp.zeros((K, channels, channels), jnp.float32)
    weight_total, outputs = lax.scan(first_pass, start_grad, tile_ids)
    activation, local_grad, halo_grad = outputs
    halo_all = halo_grad.reshape(N_GX, N_GY, N_REP, EXT_BLOCKS - NB, 128, channels)
    block_ids = jnp.arange(NB, dtype=jnp.int32)

    def second_pass(tile_id):
        pos_x, pos_y, replica = locate(tile_id)
        returned = []
        indices = []
        for slot_id, (step_x, step_y) in enumerate(face_steps):
            near_x, near_y, inside = neighbour(pos_x, pos_y, step_x, step_y)
            first_row = face_back[slot_id] * HF
            returned_piece = halo_all[near_x, near_y, replica][first_row:first_row + HF]
            returned.append(jnp.where(inside, returned_piece, jnp.zeros_like(returned_piece)))
            indices.append(face_lists[pos_x, pos_y, replica, slot_id])
        for slot_id, (step_x, step_y) in enumerate(corner_steps):
            near_x, near_y, inside = neighbour(pos_x, pos_y, step_x, step_y)
            first_row = 4 * HF + (3 - slot_id) * HC
            returned_piece = halo_all[near_x, near_y, replica][first_row:first_row + HC]
            returned.append(jnp.where(inside, returned_piece, jnp.zeros_like(returned_piece)))
            indices.append(corner_lists[pos_x, pos_y, replica, slot_id])
        gathered = jnp.concatenate(returned, 0).astype(jnp.float32)
        listed = jnp.concatenate(indices, 0)
        select = (listed[None, :] == block_ids[:, None]).astype(jnp.float32)
        block_grad = local_grad[tile_id] + jnp.einsum('bn,nrc->brc', select, gathered, precision=lax.Precision.HIGHEST)
        return block_grad.astype(jnp.bfloat16)
    input_grad = lax.map(second_pass, tile_ids)
    weight_grad = weight_total * (TILES * P_SIZE * 128) ** (-0.5)
    return (activation.reshape(-1, channels), input_grad.reshape(-1, channels), weight_grad)
```

```python
import functools

import jax
import jax.numpy as jnp
from jax import lax
from jax.experimental import pallas as pl
from jax.experimental.pallas import tpu as pltpu
from jax.sharding import PartitionSpec as P

ALL = ("gx", "gy", "rep")
K, C, NB, ROWS, PAIRS = 27, 256, 8, 128, 4
EXT = 29
KPAD = 32
BF, F32 = jnp.bfloat16, jnp.float32
VM = pl.BlockSpec(memory_space=pltpu.VMEM)
SM = pl.BlockSpec(memory_space=pltpu.SMEM)
PARAMS = pltpu.CompilerParams(vmem_limit_bytes=58 * 1024 * 1024)


def shape_of(*dims, dtype=BF):
    return jax.ShapeDtypeStruct(dims, dtype)


def call(kernel, ins, outs, scratch=(), cost=None):
    specs = [SM if kind == "s" else VM for kind, _ in ins]
    return pl.pallas_call(
        kernel,
        out_shape=outs,
        in_specs=specs,
        out_specs=[VM] * len(outs),
        scratch_shapes=list(scratch),
        compiler_params=PARAMS,
        cost_estimate=cost,
    )(*[value for _, value in ins])


def flat_id(core, x, y, z):
    return (core * 64 + ((z % 8) * 4 + y % 4) * 2 + (x % 4) // 2) * 2 + x % 2


def torus_perm(move):
    pairs = []
    for core in range(2):
        for z in range(8):
            for y in range(4):
                for x in range(4):
                    pairs.append((flat_id(core, x, y, z), flat_id(*move(core, x, y, z))))
    return pairs


def shift(value, **by):
    def move(core, x, y, z):
        return (
            (core + by.get("core", 0)) % 2,
            x + by.get("x", 0),
            y + by.get("y", 0),
            z + by.get("z", 0),
        )

    return lax.ppermute(value, ALL, torus_perm(move))


def grid_shift(value, step_x, step_y):
    pairs = []
    for i in range(2):
        for j in range(64):
            if 0 <= j + step_y < 64:
                for r in range(2):
                    to = ((i + step_x) % 2 * 64 + j + step_y) * 2 + r
                    pairs.append(((i * 64 + j) * 2 + r, to))
    return lax.ppermute(value, ALL, pairs)


def pick_kernel(core_ref, face_ref, corner_ref, feats, face_x, low_y, high_y, low_c, high_c):
    i = core_ref[0]
    for n in range(4):
        face_x[n] = feats[face_ref[(1 - i) * 4 + n]]
        low_y[n] = feats[face_ref[8 + n]]
        high_y[n] = feats[face_ref[12 + n]]
    low_c[...] = feats[corner_ref[2 * (1 - i)]]
    high_c[...] = feats[corner_ref[2 * (1 - i) + 1]]


def join_weight(core, rep, own, far, far_other, full):
    near_rows = pl.ds(pl.multiple_of(core * 128, 128), 128)
    other_rows = pl.ds(pl.multiple_of((1 - core) * 128, 128), 128)
    for side in range(2):

        @pl.when(rep == side)
        def _():
            mine = slice(side * 128, side * 128 + 128)
            theirs = slice(128 - side * 128, 256 - side * 128)

            def step(k, carry):
                full[k, :, mine] = own[k]
                full[k, near_rows, theirs] = far[k]
                full[k, other_rows, theirs] = far_other[k]
                return carry

            lax.fori_loop(0, K, step, 0)


def forward_kernel(
    meta, outs, ins, maps, feats, face_x, from_low, from_high, low_c, high_c,
    own, far, far_other, cotan,
    act, grad, keep, send,
    ext, full, rows, acc, flipped,
):
    core, rep = meta[0], meta[1]
    zeros = jnp.zeros((4, ROWS, C), BF)
    ext[0:8] = feats[...]
    ext[pl.ds(8 + 4 * (1 - core), 4)] = face_x[...]
    ext[pl.ds(8 + 4 * core, 4)] = zeros
    ext[16:20] = from_low[...]
    ext[20:24] = from_high[...]
    ext[24 + 2 * (1 - core)] = low_c[...]
    ext[25 + 2 * (1 - core)] = high_c[...]
    ext[pl.ds(24 + 2 * core, 2)] = zeros[:2]
    ext[28] = zeros[0]
    join_weight(core, rep, own, far, far_other, full)
    acc[...] = jnp.zeros_like(acc)
    places = lax.broadcasted_iota(jnp.int32, (ROWS, ROWS), 0)

    def gather_step(k, carry):
        map_k = maps[k]
        for p in range(PAIRS):
            hot = (places == map_k[p : p + 1, :]).astype(F32).astype(BF)
            picked = lax.dot_general(
                hot, ext[ins[k * PAIRS + p]], (((0,), (0,)), ((), ())), preferred_element_type=F32
            )
            rows[k, p * ROWS : (p + 1) * ROWS, :] = picked.astype(BF)
        product = jnp.dot(rows[k], full[k], preferred_element_type=F32)
        for p in range(PAIRS):
            acc[outs[k * PAIRS + p]] += product[p * ROWS : (p + 1) * ROWS]
        return carry

    lax.fori_loop(0, K, gather_step, 0)

    def grad_step(b, carry):
        value = acc[b]
        sigma = 1.0 / (1.0 + jnp.exp(-value))
        act[b] = (value * sigma).astype(BF)
        up = cotan[b].astype(F32) * (sigma * (1.0 + value * (1.0 - sigma)))
        grad[b] = up.astype(BF)
        flipped[b] = up.T.astype(BF)
        return carry

    lax.fori_loop(0, NB, grad_step, 0)

    def weight_step(k, carry):
        left = jnp.concatenate([flipped[outs[k * PAIRS + p]] for p in range(PAIRS)], axis=1)
        part = jnp.dot(left, rows[k], preferred_element_type=F32)
        for side in range(2):
            first = part[side * 128 : side * 128 + 64]
            second = part[side * 128 + 64 : side * 128 + 128]
            kept = jnp.where(core == 0, first, second).astype(BF)
            sent = jnp.where(core == 0, second, first).astype(BF)
            for y in range(4):
                keep[y, side, k] = kept[y * 16 : y * 16 + 16]
                send[y, side, k] = sent[y * 16 : y * 16 + 16]
        return carry

    lax.fori_loop(0, K, weight_step, 0)


def backward_kernel(
    meta, outs, ins, maps, grad, own, far, far_other,
    local, face_x, to_low, to_high, low_c, high_c,
    full, stack, acc,
):
    core, rep = meta[0], meta[1]
    join_weight(core, rep, own, far, far_other, full)
    acc[...] = jnp.zeros_like(acc)
    places = lax.broadcasted_iota(jnp.int32, (ROWS, ROWS), 0)

    def step(k, carry):
        map_k = maps[k]
        for p in range(PAIRS):
            hot = (places == map_k[p : p + 1, :]).astype(F32).astype(BF)
            spread = jnp.dot(hot, grad[outs[k * PAIRS + p]], preferred_element_type=F32)
            stack[p * ROWS : (p + 1) * ROWS, :] = spread.astype(BF)
        product = lax.dot_general(
            stack[...], full[k], (((1,), (1,)), ((), ())), preferred_element_type=F32
        )
        for p in range(PAIRS):
            acc[ins[k * PAIRS + p]] += product[p * ROWS : (p + 1) * ROWS]
        return carry

    lax.fori_loop(0, K, step, 0)
    local[...] = acc[0:8]
    face_x[...] = acc[pl.ds(8 + 4 * (1 - core), 4)].astype(BF)
    to_low[...] = acc[16:20].astype(BF)
    to_high[...] = acc[20:24].astype(BF)
    low_c[...] = acc[24 + 2 * (1 - core)].astype(BF)
    high_c[...] = acc[25 + 2 * (1 - core)].astype(BF)


def input_kernel(
    core_ref, face_ref, corner_ref, local, face_x, from_low, from_high, low_c, high_c, out, acc
):
    i = core_ref[0]
    acc[...] = local[...]
    for n in range(4):
        acc[face_ref[(1 - i) * 4 + n]] += face_x[n].astype(F32)
        acc[face_ref[8 + n]] += from_low[n].astype(F32)
        acc[face_ref[12 + n]] += from_high[n].astype(F32)
    acc[corner_ref[2 * (1 - i)]] += low_c[...].astype(F32)
    acc[corner_ref[2 * (1 - i) + 1]] += high_c[...].astype(F32)
    out[...] = acc[...].astype(BF)


def final_kernel(scale, meta, mine, other, out):
    core, half, y_at, z_at = meta[0], meta[2], meta[3], meta[4]

    def step(k, carry):
        z = (z_at - k // 4) & 7
        for side in range(2):
            source = (mine, other)[side]
            halves = []
            for x in range(2):
                pieces = [
                    source[(y_at - y) & 3, (half - x) & 1, z, k % 4].astype(F32) for y in range(4)
                ]
                halves.append(jnp.concatenate(pieces, 0))
            block = jnp.concatenate(halves, 1) * scale
            turned = block.T
            for first in range(2):

                @pl.when(core == first)
                def _():
                    at = 64 * (first ^ side)
                    out[k, :, at : at + 64] = turned

        return carry

    lax.fori_loop(0, K, step, 0)


def spread_ring(take, me, count, axis):
    total = take(me)
    arrived = [
        shift(take((me + s) % count).astype(BF), **{axis: s}) for s in range(1, count)
    ]
    for piece in arrived:
        total = total + piece.astype(F32)
    return total


def collect_ring(value, count, axis, stride=1):
    return jnp.stack(
        [value] + [shift(value, **{axis: s * stride}) for s in range(1, count)], 0
    )


def body(feats, weight, cotan, face_send, corner_send, pair_out, pair_in, row_map):
    core = lax.axis_index("gx")
    gy = lax.axis_index("gy")
    rep = lax.axis_index("rep")
    half, y_at, z_at = gy % 2, gy // 2 % 4, gy // 8
    x_at = half * 2 + rep
    meta = jnp.stack([core, rep, half, y_at, z_at]).astype(jnp.int32)
    blocks = feats.reshape(NB, ROWS, C)
    face = face_send.reshape(16)
    corner = corner_send.reshape(4)
    outs, ins = pair_out.reshape(-1), pair_in.reshape(-1)
    maps = row_map[0]
    four, one = shape_of(4, ROWS, C), shape_of(ROWS, C)

    face_x, low_y, high_y, low_c, high_c = call(
        pick_kernel,
        [("s", meta), ("s", face), ("s", corner), ("v", blocks)],
        [four, four, four, one, one],
    )
    from_high = grid_shift(low_y, 0, -1)
    from_low = grid_shift(high_y, 0, 1)
    from_high_c = grid_shift(low_c, 1, -1)
    from_low_c = grid_shift(high_c, 1, 1)
    from_x = grid_shift(face_x, 1, 0)
    wanted = lax.dynamic_slice_in_dim(weight, core * 128, 128, 1)
    far = lax.ppermute(
        wanted, ALL, torus_perm(lambda c, x, y, z: (c, x + (1 if c == 0 else -1), y, z))
    )
    far_other = shift(far, core=1)

    act, grad, keep, send = call(
        forward_kernel,
        [("s", meta), ("s", outs), ("s", ins), ("v", maps), ("v", blocks), ("v", from_x)]
        + [("v", v) for v in (from_low, from_high, from_low_c, from_high_c)]
        + [("v", v) for v in (weight, far, far_other, cotan.reshape(NB, ROWS, C))],
        [
            shape_of(NB, ROWS, C),
            shape_of(NB, ROWS, C),
            shape_of(4, 2, K, 16, C),
            shape_of(4, 2, K, 16, C),
        ],
        [
            pltpu.VMEM((EXT, ROWS, C), BF),
            pltpu.VMEM((K, C, C), BF),
            pltpu.VMEM((K, PAIRS * ROWS, C), BF),
            pltpu.VMEM((NB, ROWS, C), F32),
            pltpu.VMEM((NB, C, ROWS), BF),
        ],
        pl.CostEstimate(flops=7_000_000_000, bytes_accessed=12_000_000, transcendentals=0),
    )
    got = shift(send, core=1)
    local, back_x, to_low, to_high, back_low_c, back_high_c = call(
        backward_kernel,
        [("s", meta), ("s", outs), ("s", ins), ("v", maps), ("v", grad)]
        + [("v", v) for v in (weight, far, far_other)],
        [shape_of(NB, ROWS, C, dtype=F32), four, four, four, one, one],
        [
            pltpu.VMEM((K, C, C), BF),
            pltpu.VMEM((PAIRS * ROWS, C), BF),
            pltpu.VMEM((EXT, ROWS, C), F32),
        ],
        pl.CostEstimate(flops=5_000_000_000, bytes_accessed=10_000_000, transcendentals=0),
    )
    return_high = grid_shift(to_low, 0, -1)
    return_low = grid_shift(to_high, 0, 1)
    return_high_c = grid_shift(back_low_c, 1, -1)
    return_low_c = grid_shift(back_high_c, 1, 1)
    return_x = grid_shift(back_x, 1, 0)

    def take_y(n):
        return lax.dynamic_index_in_dim(keep, n, 0, False).astype(
            F32
        ) + lax.dynamic_index_in_dim(got, n, 0, False).astype(F32)

    sum_y = spread_ring(take_y, y_at, 4, "y")

    def take_x(n):
        return lax.dynamic_slice(sum_y, (n % 2, 0, 0, n // 2 * 128), (1, K, 16, 128))[0]

    sum_x = spread_ring(take_x, x_at, 4, "x")
    padded = jnp.concatenate([sum_x, jnp.zeros((KPAD - K, 16, 128), F32)], 0)

    def take_z(n):
        return lax.dynamic_slice_in_dim(padded, n * 4, 4, 0)

    sum_z = spread_ring(take_z, z_at, 8, "z")
    all_z = collect_ring(sum_z.astype(BF), 8, "z")
    all_x = collect_ring(all_z, 2, "x", 2)
    mine = collect_ring(all_x, 4, "y")
    other = shift(mine, core=1)

    input_grad = call(
        input_kernel,
        [("s", meta), ("s", face), ("s", corner), ("v", local), ("v", return_x)]
        + [("v", v) for v in (return_low, return_high, return_low_c, return_high_c)],
        [shape_of(NB, ROWS, C)],
        [pltpu.VMEM((NB, ROWS, C), F32)],
    )[0]
    tiles = lax.axis_size("gx") * lax.axis_size("gy") * lax.axis_size("rep")
    scale = float((tiles * PAIRS * ROWS) ** (-0.5))
    weight_grad = call(
        functools.partial(final_kernel, scale),
        [("s", meta), ("v", mine), ("v", other)],
        [shape_of(K, C, 128, dtype=F32)],
    )[0]
    return act.reshape(-1, C), input_grad.reshape(-1, C), weight_grad


def solution(mesh):
    tiles = ("gx", "gy", "rep")
    in_specs = (
        P(tiles, None),
        P(None, None, "rep"),
        P(tiles, None),
        P(tiles, None, None),
        P(tiles, None, None),
        P(tiles, None, None),
        P(tiles, None, None),
        P(tiles, None, None, None),
    )
    out_specs = (P(tiles, None), P(tiles, None), P(None, None, "rep"))
    return jax.shard_map(body, mesh=mesh, in_specs=in_specs, out_specs=out_specs, check_vma=False)
```

```python
import functools

import jax
import jax.numpy as jnp
from jax import lax
from jax.experimental import pallas as pl
from jax.experimental.pallas import tpu as pltpu
from jax.sharding import PartitionSpec as P

ALL = ("gx", "gy", "rep")
K, C, NB, ROWS, PAIRS = 27, 256, 8, 128, 4
EXT = 29
KPAD = 32
BF, F32 = jnp.bfloat16, jnp.float32
VM = pl.BlockSpec(memory_space=pltpu.VMEM)
SM = pl.BlockSpec(memory_space=pltpu.SMEM)
PARAMS = pltpu.CompilerParams(vmem_limit_bytes=58 * 1024 * 1024)


def shape_of(*dims, dtype=BF):
    return jax.ShapeDtypeStruct(dims, dtype)


def call(kernel, ins, outs, scratch=(), cost=None):
    place = {"s": SM, "v": VM, "a": pl.BlockSpec(memory_space=pl.ANY)}
    outs = [out if isinstance(out, tuple) else ("v", out) for out in outs]
    return pl.pallas_call(
        kernel,
        out_shape=[out for _, out in outs],
        in_specs=[place[kind] for kind, _ in ins],
        out_specs=[place[kind] for kind, _ in outs],
        scratch_shapes=list(scratch),
        compiler_params=PARAMS,
        cost_estimate=cost,
    )(*[value for _, value in ins])


def flat_id(core, x, y, z):
    return (core * 64 + ((z % 8) * 4 + y % 4) * 2 + (x % 4) // 2) * 2 + x % 2


def torus_perm(move):
    pairs = []
    for core in range(2):
        for z in range(8):
            for y in range(4):
                for x in range(4):
                    pairs.append((flat_id(core, x, y, z), flat_id(*move(core, x, y, z))))
    return pairs


def shift(value, **by):
    def move(core, x, y, z):
        return (
            (core + by.get("core", 0)) % 2,
            x + by.get("x", 0),
            y + by.get("y", 0),
            z + by.get("z", 0),
        )

    return lax.ppermute(value, ALL, torus_perm(move))


def grid_shift(value, step_x, step_y):
    pairs = []
    for i in range(2):
        for j in range(64):
            if 0 <= j + step_y < 64:
                for r in range(2):
                    to = ((i + step_x) % 2 * 64 + j + step_y) * 2 + r
                    pairs.append(((i * 64 + j) * 2 + r, to))
    return lax.ppermute(value, ALL, pairs)


def pick_kernel(core_ref, face_ref, corner_ref, feats, weight, face_x, low_y, high_y, part, sem):
    i = core_ref[0]
    rows = pl.ds(pl.multiple_of(i * 128, 128), 128)
    copy = pltpu.make_async_copy(weight.at[:, rows, :], part, sem)
    copy.start()
    for n in range(4):
        face_x[n] = feats[face_ref[(1 - i) * 4 + n]]
        low_y[n] = feats[face_ref[8 + n]]
        high_y[n] = feats[face_ref[12 + n]]
    for n in range(2):
        face_x[4 + n] = feats[corner_ref[2 * (1 - i) + n]]
    low_y[4] = face_x[4]
    high_y[4] = face_x[5]
    copy.wait()


def weight_copies(core, side, own, far, far_other, full, sems):
    near_rows = pl.ds(pl.multiple_of(core * 128, 128), 128)
    other_rows = pl.ds(pl.multiple_of((1 - core) * 128, 128), 128)
    mine = slice(side * 128, side * 128 + 128)
    theirs = slice(128 - side * 128, 256 - side * 128)
    return (
        pltpu.make_async_copy(own, full.at[:, :, mine], sems.at[0]),
        pltpu.make_async_copy(far, full.at[:, near_rows, theirs], sems.at[1]),
        pltpu.make_async_copy(far_other, full.at[:, other_rows, theirs], sems.at[2]),
    )


def on_weights(act, core, rep, *refs):
    for side in range(2):

        @pl.when(rep == side)
        def _():
            for copy in weight_copies(core, side, *refs):
                getattr(copy, act)()


def forward_kernel(
    meta, outs, ins, maps, feats, from_x, from_low, from_high, own, far, far_other, cotan,
    act, grad, keep, send,
    ext, full, rows, acc, flipped, sems,
):
    core, rep = meta[0], meta[1]
    weights = (own, far, far_other, full, sems)
    on_weights("start", core, rep, *weights)
    ext[8:16] = jnp.zeros((8, ROWS, C), BF)
    ext[24:29] = jnp.zeros((5, ROWS, C), BF)
    copies = [
        pltpu.make_async_copy(feats, ext.at[0:8], sems.at[3]),
        pltpu.make_async_copy(from_x.at[0:4], ext.at[pl.ds(8 + 4 * (1 - core), 4)], sems.at[4]),
        pltpu.make_async_copy(from_low.at[0:4], ext.at[16:20], sems.at[5]),
        pltpu.make_async_copy(from_high.at[0:4], ext.at[20:24], sems.at[6]),
        pltpu.make_async_copy(from_low.at[4], ext.at[24 + 2 * (1 - core)], sems.at[7]),
        pltpu.make_async_copy(from_high.at[4], ext.at[25 + 2 * (1 - core)], sems.at[8]),
    ]
    for copy in copies:
        copy.start()
    acc[...] = jnp.zeros_like(acc)
    places = lax.broadcasted_iota(jnp.int32, (ROWS, ROWS), 0)
    for copy in copies:
        copy.wait()
    on_weights("wait", core, rep, *weights)

    def gather_step(k, carry):
        map_k = maps[k]
        for p in range(PAIRS):
            hot = (places == map_k[p : p + 1, :]).astype(F32).astype(BF)
            picked = lax.dot_general(
                hot, ext[ins[k * PAIRS + p]], (((0,), (0,)), ((), ())), preferred_element_type=F32
            )
            rows[k, p * ROWS : (p + 1) * ROWS, :] = picked.astype(BF)
        product = jnp.dot(rows[k], full[k], preferred_element_type=F32)
        for p in range(PAIRS):
            acc[outs[k * PAIRS + p]] += product[p * ROWS : (p + 1) * ROWS]
        return carry

    lax.fori_loop(0, K, gather_step, 0, unroll=3)

    def grad_step(b, carry):
        value = acc[b]
        sigma = 1.0 / (1.0 + jnp.exp(-value))
        act[b] = (value * sigma).astype(BF)
        up = cotan[b].astype(F32) * (sigma * (1.0 + value * (1.0 - sigma)))
        grad[b] = up.astype(BF)
        flipped[b] = up.T.astype(BF)
        return carry

    lax.fori_loop(0, NB, grad_step, 0)

    def weight_step(k, carry):
        left = jnp.concatenate([flipped[outs[k * PAIRS + p]] for p in range(PAIRS)], axis=1)
        part = jnp.dot(left, rows[k], preferred_element_type=F32)
        for side in range(2):
            first = part[side * 128 : side * 128 + 64]
            second = part[side * 128 + 64 : side * 128 + 128]
            kept = jnp.where(core == 0, first, second).astype(BF)
            sent = jnp.where(core == 0, second, first).astype(BF)
            for y in range(4):
                for x in range(2):
                    at = (slice(y * 16, y * 16 + 16), slice(x * 128, x * 128 + 128))
                    keep[y * 4 + side * 2 + x, k] = kept[at]
                    send[y * 4 + side * 2 + x, k] = sent[at]
        return carry

    lax.fori_loop(0, K, weight_step, 0, unroll=3)


def backward_kernel(
    meta, outs, ins, maps, grad, own, far, far_other,
    local, face_x, to_low, to_high,
    full, acc, sems,
):
    core, rep = meta[0], meta[1]
    weights = (own, far, far_other, full, sems)
    on_weights("start", core, rep, *weights)
    acc[...] = jnp.zeros_like(acc)
    places = lax.broadcasted_iota(jnp.int32, (ROWS, ROWS), 0)
    on_weights("wait", core, rep, *weights)

    def step(k, carry):
        map_k = maps[k]
        parts = []
        for p in range(PAIRS):
            hot = (places == map_k[p : p + 1, :]).astype(F32).astype(BF)
            spread = jnp.dot(hot, grad[outs[k * PAIRS + p]], preferred_element_type=F32)
            parts.append(spread.astype(BF))
        product = lax.dot_general(
            jnp.concatenate(parts, 0), full[k], (((1,), (1,)), ((), ())), preferred_element_type=F32
        )
        for p in range(PAIRS):
            acc[ins[k * PAIRS + p]] += product[p * ROWS : (p + 1) * ROWS]
        return carry

    lax.fori_loop(0, K, step, 0, unroll=3)
    local[...] = acc[0:8]
    face_x[0:4] = acc[pl.ds(8 + 4 * (1 - core), 4)].astype(BF)
    face_x[4:6] = jnp.zeros((2, ROWS, C), BF)
    to_low[0:4] = acc[16:20].astype(BF)
    to_low[4] = acc[24 + 2 * (1 - core)].astype(BF)
    to_high[0:4] = acc[20:24].astype(BF)
    to_high[4] = acc[25 + 2 * (1 - core)].astype(BF)


def input_kernel(core_ref, face_ref, corner_ref, local, from_x, from_low, from_high, out, acc):
    i = core_ref[0]
    acc[...] = local[...]
    for n in range(4):
        acc[face_ref[(1 - i) * 4 + n]] += from_x[n].astype(F32)
        acc[face_ref[8 + n]] += from_low[n].astype(F32)
        acc[face_ref[12 + n]] += from_high[n].astype(F32)
    for n in range(2):
        acc[corner_ref[2 * (1 - i) + n]] += from_x[4 + n].astype(F32)
    out[...] = acc[...].astype(BF)


def pair_kernel(keep, got, after, out):
    def step(n, carry):
        out[n] = (keep[n].astype(F32) + got[n].astype(F32)).astype(BF)
        return carry

    lax.fori_loop(0, 16, step, 0)


def final_kernel(scale, meta, mine, other, out):
    core, half, y_at = meta[0], meta[2], meta[3]

    def step(k, carry):
        sides = []
        for source in (mine, other):
            halves = []
            for x in range(2):
                pieces = [
                    source[(y_at - y) & 3, (half - x) & 1, k // 4, k % 4].astype(F32)
                    for y in range(4)
                ]
                halves.append(jnp.concatenate(pieces, 0))
            sides.append(jnp.concatenate(halves, 1) * scale)
        first = jnp.where(core == 0, sides[0], sides[1])
        second = jnp.where(core == 0, sides[1], sides[0])
        out[k] = jnp.concatenate([first, second], 0).T
        return carry

    lax.fori_loop(0, K, step, 0, unroll=3)


def members(key):
    found = {}
    for y in range(4):
        for rep in range(2):
            for half in range(2):
                for z in range(8):
                    for core in range(2):
                        x = half * 2 + rep
                        found.setdefault(key(core, x, y, z), []).append(flat_id(core, x, y, z))
    return list(found.values())


def exchange(value, key):
    return lax.all_to_all(
        value, ALL, split_axis=0, concat_axis=0, axis_index_groups=members(key), tiled=False
    )


def collect_ring(value, count, axis, stride=1):
    return jnp.stack(
        [value] + [shift(value, **{axis: s * stride}) for s in range(1, count)], 0
    )


def body(feats, weight, cotan, face_send, corner_send, pair_out, pair_in, row_map):
    core = lax.axis_index("gx")
    gy = lax.axis_index("gy")
    rep = lax.axis_index("rep")
    half, y_at, z_at = gy % 2, gy // 2 % 4, gy // 8
    meta = jnp.stack([core, rep, half, y_at, z_at]).astype(jnp.int32)
    blocks = feats.reshape(NB, ROWS, C)
    face = face_send.reshape(16)
    corner = corner_send.reshape(4)
    outs, ins = pair_out.reshape(-1), pair_in.reshape(-1)
    maps = row_map[0]
    five, six = shape_of(5, ROWS, C), shape_of(6, ROWS, C)

    face_x, low_y, high_y, part = call(
        pick_kernel,
        [("s", meta), ("s", face), ("s", corner), ("v", blocks), ("a", weight)],
        [six, five, five, shape_of(K, 128, 128)],
        [pltpu.SemaphoreType.DMA],
    )
    from_x = grid_shift(face_x, 1, 0)
    low_y = lax.dynamic_update_slice(low_y, from_x[4:5], (4, 0, 0))
    high_y = lax.dynamic_update_slice(high_y, from_x[5:6], (4, 0, 0))
    from_high = grid_shift(low_y, 0, -1)
    from_low = grid_shift(high_y, 0, 1)
    far = lax.ppermute(
        part, ALL, torus_perm(lambda c, x, y, z: (c, x + (1 if c == 0 else -1), y, z))
    )
    far_other = shift(far, core=1)

    act, grad, keep, send = call(
        forward_kernel,
        [("s", meta), ("s", outs), ("s", ins), ("v", maps)]
        + [("a", v) for v in (blocks, from_x, from_low, from_high, weight, far, far_other)]
        + [("v", cotan.reshape(NB, ROWS, C))],
        [
            shape_of(NB, ROWS, C),
            shape_of(NB, ROWS, C),
            shape_of(16, K, 16, 128),
            shape_of(16, K, 16, 128),
        ],
        [
            pltpu.VMEM((EXT, ROWS, C), BF),
            pltpu.VMEM((K, C, C), BF),
            pltpu.VMEM((K, PAIRS * ROWS, C), BF),
            pltpu.VMEM((NB, ROWS, C), F32),
            pltpu.VMEM((NB, C, ROWS), BF),
            pltpu.SemaphoreType.DMA((9,)),
        ],
        pl.CostEstimate(flops=7_000_000_000, bytes_accessed=12_000_000, transcendentals=0),
    )
    got = shift(send, core=1)
    local, back_x, to_low, to_high = call(
        backward_kernel,
        [("s", meta), ("s", outs), ("s", ins), ("v", maps), ("v", grad)]
        + [("a", v) for v in (weight, far, far_other)],
        [shape_of(NB, ROWS, C, dtype=F32), six, five, five],
        [
            pltpu.VMEM((K, C, C), BF),
            pltpu.VMEM((EXT, ROWS, C), F32),
            pltpu.SemaphoreType.DMA((3,)),
        ],
        pl.CostEstimate(flops=5_000_000_000, bytes_accessed=10_000_000, transcendentals=0),
    )
    return_high = grid_shift(to_low, 0, -1)
    return_low = grid_shift(to_high, 0, 1)
    back_x = lax.dynamic_update_slice(back_x, return_low[4:5], (4, 0, 0))
    back_x = lax.dynamic_update_slice(back_x, return_high[4:5], (5, 0, 0))
    return_x = grid_shift(back_x, 1, 0)

    paired = call(
        pair_kernel,
        [("v", keep), ("v", got), ("a", to_low)],
        [shape_of(16, K, 16, 128)],
    )[0]
    spread = exchange(paired, lambda c, x, y, z: (c, z))
    sum_xy = jnp.sum(spread.astype(F32), 0)
    padded = jnp.concatenate([sum_xy, jnp.zeros((KPAD - K, 16, 128), F32)], 0)
    spread = exchange(padded.astype(BF).reshape(8, 4, 16, 128), lambda c, x, y, z: (c, x, y))
    sum_z = jnp.sum(spread.astype(F32), 0).astype(BF)
    all_z = exchange(jnp.broadcast_to(sum_z, (8, 4, 16, 128)), lambda c, x, y, z: (c, x, y))
    all_x = collect_ring(all_z, 2, "x", 2)
    mine = collect_ring(all_x, 4, "y")
    other = shift(mine, core=1)

    input_grad = call(
        input_kernel,
        [("s", meta), ("s", face), ("s", corner), ("v", local), ("v", return_x)]
        + [("v", v) for v in (return_low, return_high)],
        [shape_of(NB, ROWS, C)],
        [pltpu.VMEM((NB, ROWS, C), F32)],
    )[0]
    tiles = lax.axis_size("gx") * lax.axis_size("gy") * lax.axis_size("rep")
    scale = float((tiles * PAIRS * ROWS) ** (-0.5))
    weight_grad = call(
        functools.partial(final_kernel, scale),
        [("s", meta), ("v", mine), ("v", other)],
        [shape_of(K, C, 128, dtype=F32)],
    )[0]
    return act.reshape(-1, C), input_grad.reshape(-1, C), weight_grad


def solution(mesh):
    tiles = ("gx", "gy", "rep")
    in_specs = (
        P(tiles, None),
        P(None, None, "rep"),
        P(tiles, None),
        P(tiles, None, None),
        P(tiles, None, None),
        P(tiles, None, None),
        P(tiles, None, None),
        P(tiles, None, None, None),
    )
    out_specs = (P(tiles, None), P(tiles, None), P(None, None, "rep"))
    return jax.shard_map(body, mesh=mesh, in_specs=in_specs, out_specs=out_specs, check_vma=False)
```

```python
import functools

import jax
import jax.numpy as jnp
from jax import lax
from jax.experimental import pallas as pl
from jax.experimental.pallas import tpu as pltpu
from jax.sharding import PartitionSpec as P

ALL = ("gx", "gy", "rep")
K, C, NB, ROWS, PAIRS = 27, 256, 8, 128, 4
EXT = 29
KPAD = 32
BF, F32 = jnp.bfloat16, jnp.float32
VM = pl.BlockSpec(memory_space=pltpu.VMEM)
SM = pl.BlockSpec(memory_space=pltpu.SMEM)
PARAMS = pltpu.CompilerParams(vmem_limit_bytes=26 * 1024 * 1024)


def shape_of(*dims, dtype=BF):
    return jax.ShapeDtypeStruct(dims, dtype)


def call(kernel, ins, outs, scratch=(), cost=None):
    place = {"s": SM, "v": VM, "a": pl.BlockSpec(memory_space=pl.ANY)}
    outs = [out if isinstance(out, tuple) else ("v", out) for out in outs]
    return pl.pallas_call(
        kernel,
        out_shape=[out for _, out in outs],
        in_specs=[place[kind] for kind, _ in ins],
        out_specs=[place[kind] for kind, _ in outs],
        scratch_shapes=list(scratch),
        compiler_params=PARAMS,
        cost_estimate=cost,
    )(*[value for _, value in ins])


def tie(value, *after):
    return lax.optimization_barrier((value, *after))[0]


def places():
    gy = lax.axis_index("gy")
    return lax.axis_index("gx"), lax.axis_index("rep"), gy % 2, gy // 2 % 4, gy // 8


def flat_id(core, x, y, z):
    return (core * 64 + ((z % 8) * 4 + y % 4) * 2 + (x % 4) // 2) * 2 + x % 2


def torus_perm(move):
    pairs = []
    for core in range(2):
        for z in range(8):
            for y in range(4):
                for x in range(4):
                    pairs.append((flat_id(core, x, y, z), flat_id(*move(core, x, y, z))))
    return pairs


def shift(value, **by):
    def move(core, x, y, z):
        return (
            (core + by.get("core", 0)) % 2,
            x + by.get("x", 0),
            y + by.get("y", 0),
            z + by.get("z", 0),
        )

    return lax.ppermute(value, ALL, torus_perm(move))


def grid_shift(value, step_x, step_y):
    pairs = []
    for i in range(2):
        for j in range(64):
            if 0 <= j + step_y < 64:
                for r in range(2):
                    to = ((i + step_x) % 2 * 64 + j + step_y) * 2 + r
                    pairs.append(((i * 64 + j) * 2 + r, to))
    return lax.ppermute(value, ALL, pairs)


def pick_kernel(face, corner, feats, face_x, low_y, high_y):
    i = lax.axis_index("gx")
    for n in range(4):
        face_x[n] = feats[face[0, 1 - i, n]]
        low_y[n] = feats[face[0, 2, n]]
        high_y[n] = feats[face[0, 3, n]]
    for n in range(2):
        face_x[4 + n] = feats[corner[0, 0, 2 * (1 - i) + n]]
    low_y[4] = face_x[4]
    high_y[4] = face_x[5]


def weight_copies(core, side, own, far, far_other, full, sems):
    near_rows = pl.ds(pl.multiple_of(core * 128, 128), 128)
    other_rows = pl.ds(pl.multiple_of((1 - core) * 128, 128), 128)
    mine = slice(side * 128, side * 128 + 128)
    theirs = slice(128 - side * 128, 256 - side * 128)
    return (
        pltpu.make_async_copy(own, full.at[:, :, mine], sems.at[0]),
        pltpu.make_async_copy(far, full.at[:, near_rows, theirs], sems.at[1]),
        pltpu.make_async_copy(far_other, full.at[:, other_rows, theirs], sems.at[2]),
    )


def on_weights(act, core, rep, *refs):
    for side in range(2):

        @pl.when(rep == side)
        def _():
            for copy in weight_copies(core, side, *refs):
                getattr(copy, act)()


def forward_kernel(
    outs, ins, maps, feats, from_x, from_low, from_high, own, far, far_other, cotan,
    act, grad, keep, send,
    ext, full, rows, acc, flipped, sems,
):
    core, rep = places()[:2]
    weights = (own, far, far_other, full, sems)
    on_weights("start", core, rep, *weights)
    ext[8:16] = jnp.zeros((8, ROWS, C), BF)
    ext[24:29] = jnp.zeros((5, ROWS, C), BF)
    copies = [
        pltpu.make_async_copy(feats, ext.at[0:8], sems.at[3]),
        pltpu.make_async_copy(from_x.at[0:4], ext.at[pl.ds(8 + 4 * (1 - core), 4)], sems.at[4]),
        pltpu.make_async_copy(from_low.at[0:4], ext.at[16:20], sems.at[5]),
        pltpu.make_async_copy(from_high.at[0:4], ext.at[20:24], sems.at[6]),
        pltpu.make_async_copy(from_low.at[4], ext.at[24 + 2 * (1 - core)], sems.at[7]),
        pltpu.make_async_copy(from_high.at[4], ext.at[25 + 2 * (1 - core)], sems.at[8]),
    ]
    for copy in copies:
        copy.start()
    acc[...] = jnp.zeros_like(acc)
    lanes = lax.broadcasted_iota(jnp.int32, (ROWS, ROWS), 0)
    for copy in copies:
        copy.wait()

    def gather_step(k, carry):
        map_k = maps[k]
        for p in range(PAIRS):
            hot = (lanes == map_k[p : p + 1, :]).astype(F32).astype(BF)
            picked = lax.dot_general(
                hot, ext[ins[0, p, k]], (((0,), (0,)), ((), ())), preferred_element_type=F32
            )
            rows[k, p * ROWS : (p + 1) * ROWS, :] = picked.astype(BF)
        return carry

    lax.fori_loop(0, K, gather_step, 0, unroll=27)
    on_weights("wait", core, rep, *weights)

    def product_step(k, carry):
        product = jnp.dot(rows[k], full[k], preferred_element_type=F32)
        for p in range(PAIRS):
            acc[outs[0, p, k]] += product[p * ROWS : (p + 1) * ROWS]
        return carry

    lax.fori_loop(0, K, product_step, 0, unroll=27)

    def grad_step(b, carry):
        value = acc[b]
        sigma = 1.0 / (1.0 + jnp.exp(-value))
        act[b] = (value * sigma).astype(BF)
        up = cotan[b].astype(F32) * (sigma * (1.0 + value * (1.0 - sigma)))
        grad[b] = up.astype(BF)
        flipped[b] = up.T.astype(BF)
        return carry

    lax.fori_loop(0, NB, grad_step, 0, unroll=4)

    def weight_step(k, carry):
        left = jnp.concatenate([flipped[outs[0, p, k]] for p in range(PAIRS)], axis=1)
        part = jnp.dot(left, rows[k], preferred_element_type=F32)
        for side in range(2):
            first = part[side * 128 : side * 128 + 64]
            second = part[side * 128 + 64 : side * 128 + 128]
            kept = jnp.where(core == 0, first, second).astype(BF)
            sent = jnp.where(core == 0, second, first).astype(BF)
            for y in range(4):
                for x in range(2):
                    at = (slice(y * 16, y * 16 + 16), slice(x * 128, x * 128 + 128))
                    keep[y * 4 + side * 2 + x, k] = kept[at]
                    send[y * 4 + side * 2 + x, k] = sent[at]
        return carry

    lax.fori_loop(0, K, weight_step, 0, unroll=27)


def backward_kernel(
    outs, ins, maps, grad, own, far, far_other,
    local, face_x, to_low, to_high,
    full, rows, acc, sems,
):
    core, rep = places()[:2]
    weights = (own, far, far_other, full, sems)
    on_weights("start", core, rep, *weights)
    acc[...] = jnp.zeros_like(acc)
    lanes = lax.broadcasted_iota(jnp.int32, (ROWS, ROWS), 0)

    def spread_step(k, carry):
        map_k = maps[k]
        for p in range(PAIRS):
            hot = (lanes == map_k[p : p + 1, :]).astype(F32).astype(BF)
            spread = jnp.dot(hot, grad[outs[0, p, k]], preferred_element_type=F32)
            rows[k, p * ROWS : (p + 1) * ROWS, :] = spread.astype(BF)
        return carry

    lax.fori_loop(0, K, spread_step, 0, unroll=27)
    on_weights("wait", core, rep, *weights)

    def step(k, carry):
        product = lax.dot_general(
            rows[k], full[k], (((1,), (1,)), ((), ())), preferred_element_type=F32
        )
        for p in range(PAIRS):
            acc[ins[0, p, k]] += product[p * ROWS : (p + 1) * ROWS]
        return carry

    lax.fori_loop(0, K, step, 0, unroll=27)
    local[...] = acc[0:8]
    face_x[0:4] = acc[pl.ds(8 + 4 * (1 - core), 4)].astype(BF)
    face_x[4:6] = jnp.zeros((2, ROWS, C), BF)
    to_low[0:4] = acc[16:20].astype(BF)
    to_low[4] = acc[24 + 2 * (1 - core)].astype(BF)
    to_high[0:4] = acc[20:24].astype(BF)
    to_high[4] = acc[25 + 2 * (1 - core)].astype(BF)


def input_kernel(face, corner, local, from_x, from_low, from_high, out, acc):
    i = lax.axis_index("gx")
    acc[...] = local[...]
    for n in range(4):
        acc[face[0, 1 - i, n]] += from_x[n].astype(F32)
        acc[face[0, 2, n]] += from_low[n].astype(F32)
        acc[face[0, 3, n]] += from_high[n].astype(F32)
    for n in range(2):
        acc[corner[0, 0, 2 * (1 - i) + n]] += from_x[4 + n].astype(F32)
    out[...] = acc[...].astype(BF)


def final_kernel(scale, *refs):
    core, _, _, y_at, _ = places()
    out = refs[8]
    first = pl.program_id(0) * 9

    def run(turn):
        def step(n, carry):
            k = first + n
            sides = []
            for side in range(2):
                halves = []
                for x in range(2):
                    pieces = [refs[side * 4 + (turn - y) % 4][x, k].astype(F32) for y in range(4)]
                    halves.append(jnp.concatenate(pieces, 0))
                sides.append(jnp.concatenate(halves, 1) * scale)
            low = jnp.where(core == 0, sides[0], sides[1])
            high = jnp.where(core == 0, sides[1], sides[0])
            out[n] = jnp.concatenate([low, high], 0).T
            return carry

        lax.fori_loop(0, 9, step, 0, unroll=3)

    for turn in range(4):
        pl.when(y_at == turn)(functools.partial(run, turn))


def members(key):
    found = {}
    for y in range(4):
        for rep in range(2):
            for half in range(2):
                for z in range(8):
                    for core in range(2):
                        x = half * 2 + rep
                        found.setdefault(key(core, x, y, z), []).append(flat_id(core, x, y, z))
    return list(found.values())


def exchange(value, key):
    return lax.all_to_all(
        value, ALL, split_axis=0, concat_axis=0, axis_index_groups=members(key), tiled=False
    )


def body(feats, weight, cotan, face_send, corner_send, pair_out, pair_in, row_map):
    blocks = feats.reshape(NB, ROWS, C)
    lists = [("s", face_send), ("s", corner_send.swapaxes(1, 2))]
    pairs = [("s", v.swapaxes(1, 2)) for v in (pair_out, pair_in)] + [("v", row_map[0])]
    five, six = shape_of(5, ROWS, C), shape_of(6, ROWS, C)

    face_x, low_y, high_y = call(pick_kernel, lists + [("v", blocks)], [six, five, five])
    from_x = grid_shift(face_x, 1, 0)
    low_y = lax.dynamic_update_slice(low_y, from_x[4:5], (4, 0, 0))
    high_y = lax.dynamic_update_slice(high_y, from_x[5:6], (4, 0, 0))
    from_high = grid_shift(low_y, 0, -1)
    from_low = grid_shift(high_y, 0, 1)
    part = lax.dynamic_slice_in_dim(weight, lax.axis_index("gx") * 128, 128, 1)
    far = lax.ppermute(
        tie(part, from_x), ALL, torus_perm(lambda c, x, y, z: (c, x + (1 if c == 0 else -1), y, z))
    )
    far = tie(far, from_high, from_low)
    far_other = shift(far, core=1)

    act, grad, keep, send = call(
        forward_kernel,
        pairs
        + [("a", v) for v in (blocks, from_x, from_low, from_high, weight, far, far_other)]
        + [("v", cotan.reshape(NB, ROWS, C))],
        [
            shape_of(NB, ROWS, C),
            shape_of(NB, ROWS, C),
            shape_of(16, K, 16, 128),
            shape_of(16, K, 16, 128),
        ],
        [
            pltpu.VMEM((EXT, ROWS, C), BF),
            pltpu.VMEM((K, C, C), BF),
            pltpu.VMEM((K, PAIRS * ROWS, C), BF),
            pltpu.VMEM((NB, ROWS, C), F32),
            pltpu.VMEM((NB, C, ROWS), BF),
            pltpu.SemaphoreType.DMA((9,)),
        ],
        pl.CostEstimate(flops=7_000_000_000, bytes_accessed=12_000_000, transcendentals=0),
    )
    got = shift(send, core=1)
    local, back_x, to_low, to_high = call(
        backward_kernel,
        pairs
        + [("v", grad)]
        + [("a", v) for v in (weight, far, far_other)],
        [shape_of(NB, ROWS, C, dtype=F32), six, five, five],
        [
            pltpu.VMEM((K, C, C), BF),
            pltpu.VMEM((K, PAIRS * ROWS, C), BF),
            pltpu.VMEM((EXT, ROWS, C), F32),
            pltpu.SemaphoreType.DMA((3,)),
        ],
        pl.CostEstimate(flops=5_000_000_000, bytes_accessed=10_000_000, transcendentals=0),
    )
    paired = (tie(keep, to_low).astype(F32) + got.astype(F32)).astype(BF)
    spread = exchange(paired, lambda c, x, y, z: (c, z))
    return_high = grid_shift(tie(to_low, spread), 0, -1)
    return_low = grid_shift(tie(to_high, spread), 0, 1)
    sum_xy = jnp.sum(spread.astype(F32), 0)
    padded = jnp.concatenate([sum_xy, jnp.zeros((KPAD - K, 16, 128), F32)], 0)
    spread = exchange(padded.astype(BF).reshape(8, 4, 16, 128), lambda c, x, y, z: (c, x, y))
    sum_z = jnp.sum(spread.astype(F32), 0).astype(BF)
    all_x = exchange(jnp.broadcast_to(sum_z, (16, 4, 16, 128)), lambda c, x, y, z: (c, x % 2, y))
    all_x = all_x.reshape(2, KPAD, 16, 128)[:, :K]
    back_x = lax.dynamic_update_slice(back_x, return_low[4:5], (4, 0, 0))
    back_x = lax.dynamic_update_slice(back_x, return_high[4:5], (5, 0, 0))
    return_x = grid_shift(back_x, 1, 0)
    mine = [all_x] + [shift(all_x, y=s) for s in range(1, 4)]
    other = [shift(tie(piece, return_low, return_high), core=1) for piece in mine]

    input_grad = call(
        input_kernel,
        lists + [("v", v) for v in (local, return_x, return_low, return_high)],
        [shape_of(NB, ROWS, C)],
        [pltpu.VMEM((NB, ROWS, C), F32)],
    )[0]
    tiles = lax.axis_size("gx") * lax.axis_size("gy") * lax.axis_size("rep")
    scale = float((tiles * PAIRS * ROWS) ** (-0.5))
    pieces = mine + other
    weight_grad = pl.pallas_call(
        functools.partial(final_kernel, scale),
        grid=(3,),
        out_shape=shape_of(K, C, 128, dtype=F32),
        in_specs=[pl.BlockSpec((2, K, 16, 128), lambda n: (0, 0, 0, 0))] * 8,
        out_specs=pl.BlockSpec((9, C, 128), lambda n: (n, 0, 0)),
        compiler_params=PARAMS,
    )(*pieces)
    return act.reshape(-1, C), input_grad.reshape(-1, C), weight_grad


def solution(mesh):
    tiles = ("gx", "gy", "rep")
    in_specs = (
        P(tiles, None),
        P(None, None, "rep"),
        P(tiles, None),
        P(tiles, None, None),
        P(tiles, None, None),
        P(tiles, None, None),
        P(tiles, None, None),
        P(tiles, None, None, None),
    )
    out_specs = (P(tiles, None), P(tiles, None), P(None, None, "rep"))
    return jax.shard_map(body, mesh=mesh, in_specs=in_specs, out_specs=out_specs, check_vma=False)
```

```python
import functools

import jax
import jax.numpy as jnp
from jax import lax
from jax.experimental import pallas as pl
from jax.experimental.pallas import tpu as pltpu
from jax.sharding import PartitionSpec as P

ALL = ("gx", "gy", "rep")
K, C, NB, ROWS, PAIRS = 27, 256, 8, 128, 4
EXT = 29
KPAD = 32
BF, F32 = jnp.bfloat16, jnp.float32
VM = pl.BlockSpec(memory_space=pltpu.VMEM)
SM = pl.BlockSpec(memory_space=pltpu.SMEM)
PARAMS = pltpu.CompilerParams(vmem_limit_bytes=26 * 1024 * 1024)


def shape_of(*dims, dtype=BF):
    return jax.ShapeDtypeStruct(dims, dtype)


def call(kernel, ins, outs, scratch=(), cost=None):
    place = {
        "s": SM,
        "v": VM,
        "a": pl.BlockSpec(memory_space=pl.ANY),
        "h": pl.BlockSpec(memory_space=pltpu.HBM),
    }
    outs = [out if isinstance(out, tuple) else ("v", out) for out in outs]
    return pl.pallas_call(
        kernel,
        out_shape=[out for _, out in outs],
        in_specs=[place[kind] for kind, _ in ins],
        out_specs=[place[kind] for kind, _ in outs],
        scratch_shapes=list(scratch),
        compiler_params=PARAMS,
        cost_estimate=cost,
    )(*[value for _, value in ins])


def tie(value, *after):
    return lax.optimization_barrier((value, *after))[0]


def places():
    gy = lax.axis_index("gy")
    return lax.axis_index("gx"), lax.axis_index("rep"), gy % 2, gy // 2 % 4, gy // 8


def flat_id(core, x, y, z):
    return (core * 64 + ((z % 8) * 4 + y % 4) * 2 + (x % 4) // 2) * 2 + x % 2


def torus_perm(move):
    pairs = []
    for core in range(2):
        for z in range(8):
            for y in range(4):
                for x in range(4):
                    pairs.append((flat_id(core, x, y, z), flat_id(*move(core, x, y, z))))
    return pairs


def shift(value, **by):
    def move(core, x, y, z):
        return (
            (core + by.get("core", 0)) % 2,
            x + by.get("x", 0),
            y + by.get("y", 0),
            z + by.get("z", 0),
        )

    return lax.ppermute(value, ALL, torus_perm(move))


def swap_y(value, which):
    pairs = []
    for j in range(64):
        to = (j ^ 1) if which == 0 else (j + 1 if j % 2 else j - 1)
        if 0 <= to < 64:
            pairs += [((i * 64 + j) * 2 + r, (i * 64 + to) * 2 + r) for i in (0, 1) for r in (0, 1)]
    return lax.ppermute(value, ALL, pairs)


def ends():
    return lax.axis_index("gx"), 1 - lax.axis_index("gy") % 2


def pick_kernel(face, corner, feats, face_x, first, second):
    i, even = ends()
    for n in range(4):
        face_x[n] = feats[face[0, 1 - i, n]]
        first[n] = feats[face[0, 2 + even, n]]
        second[n] = feats[face[0, 3 - even, n]]
    face_x[4] = feats[corner[0, 0, 2 * (1 - i) + even]]
    face_x[5] = feats[corner[0, 0, 2 * (1 - i) + 1 - even]]
    first[4] = face_x[4]
    second[4] = face_x[5]


def weight_copies(core, side, own, far, far_other, full, sems):
    near_rows = pl.ds(pl.multiple_of(core * 128, 128), 128)
    other_rows = pl.ds(pl.multiple_of((1 - core) * 128, 128), 128)
    mine = slice(side * 128, side * 128 + 128)
    theirs = slice(128 - side * 128, 256 - side * 128)
    return (
        pltpu.make_async_copy(own, full.at[:, :, mine], sems.at[0]),
        pltpu.make_async_copy(far, full.at[:, near_rows, theirs], sems.at[1]),
        pltpu.make_async_copy(far_other, full.at[:, other_rows, theirs], sems.at[2]),
    )


def on_weights(act, core, rep, *refs):
    for side in range(2):

        @pl.when(rep == side)
        def _():
            for copy in weight_copies(core, side, *refs):
                getattr(copy, act)()


def gather_kernel(ins, maps, feats, from_x, first, second, rows, ext, sems):
    core, even = ends()
    ext[8:16] = jnp.zeros((8, ROWS, C), BF)
    ext[24:29] = jnp.zeros((5, ROWS, C), BF)
    corners = 24 + 2 * (1 - core)
    copies = [
        pltpu.make_async_copy(feats, ext.at[0:8], sems.at[0]),
        pltpu.make_async_copy(from_x.at[0:4], ext.at[pl.ds(8 + 4 * (1 - core), 4)], sems.at[1]),
        pltpu.make_async_copy(first.at[0:4], ext.at[pl.ds(16 + 4 * even, 4)], sems.at[2]),
        pltpu.make_async_copy(second.at[0:4], ext.at[pl.ds(20 - 4 * even, 4)], sems.at[3]),
        pltpu.make_async_copy(first.at[4], ext.at[corners + even], sems.at[4]),
        pltpu.make_async_copy(second.at[4], ext.at[corners + 1 - even], sems.at[5]),
    ]
    for copy in copies:
        copy.start()
    lanes = lax.broadcasted_iota(jnp.int32, (ROWS, ROWS), 0)
    for copy in copies:
        copy.wait()

    def step(k, carry):
        map_k = maps[k]
        for p in range(PAIRS):
            hot = (lanes == map_k[p : p + 1, :]).astype(F32).astype(BF)
            picked = lax.dot_general(
                hot, ext[ins[0, p, k]], (((0,), (0,)), ((), ())), preferred_element_type=F32
            )
            rows[k, p * ROWS : (p + 1) * ROWS, :] = picked.astype(BF)
        return carry

    lax.fori_loop(0, K, step, 0, unroll=27)


def forward_kernel(
    outs, rows, own, far, far_other, cotan_in,
    act, grad, keep, send,
    full, acc, flipped, cotan, sems,
):
    core, rep = places()[:2]
    weights = (own, far, far_other, full, sems)
    on_weights("start", core, rep, *weights)
    cotan_copy = pltpu.make_async_copy(cotan_in, cotan, sems.at[3])
    cotan_copy.start()
    acc[...] = jnp.zeros_like(acc)
    on_weights("wait", core, rep, *weights)

    def product_step(k, carry):
        product = jnp.dot(rows[k], full[k], preferred_element_type=F32)
        for p in range(PAIRS):
            acc[outs[0, p, k]] += product[p * ROWS : (p + 1) * ROWS]
        return carry

    lax.fori_loop(0, K, product_step, 0, unroll=27)

    cotan_copy.wait()

    def grad_step(b, carry):
        value = acc[b]
        sigma = 1.0 / (1.0 + jnp.exp(-value))
        act[b] = (value * sigma).astype(BF)
        up = cotan[b].astype(F32) * (sigma * (1.0 + value * (1.0 - sigma)))
        grad[b] = up.astype(BF)
        flipped[b] = up.T.astype(BF)
        return carry

    lax.fori_loop(0, NB, grad_step, 0, unroll=4)

    def weight_step(k, carry):
        left = jnp.concatenate([flipped[outs[0, p, k]] for p in range(PAIRS)], axis=1)
        part = jnp.dot(left, rows[k], preferred_element_type=F32)
        for side in range(2):
            first = part[side * 128 : side * 128 + 64]
            second = part[side * 128 + 64 : side * 128 + 128]
            kept = jnp.where(core == 0, first, second).astype(BF)
            sent = jnp.where(core == 0, second, first).astype(BF)
            for y in range(4):
                for x in range(2):
                    at = (slice(y * 16, y * 16 + 16), slice(x * 128, x * 128 + 128))
                    keep[y * 4 + side * 2 + x, k] = kept[at]
                    send[y * 4 + side * 2 + x, k] = sent[at]
        return carry

    lax.fori_loop(0, K, weight_step, 0, unroll=27)


def backward_kernel(
    outs, ins, maps, grad, own, far, far_other,
    local, face_x, first, second,
    full, rows, acc, sems,
):
    core, rep = places()[:2]
    weights = (own, far, far_other, full, sems)
    on_weights("start", core, rep, *weights)
    acc[...] = jnp.zeros_like(acc)
    lanes = lax.broadcasted_iota(jnp.int32, (ROWS, ROWS), 0)

    def spread_step(k, carry):
        map_k = maps[k]
        for p in range(PAIRS):
            hot = (lanes == map_k[p : p + 1, :]).astype(F32).astype(BF)
            spread = jnp.dot(hot, grad[outs[0, p, k]], preferred_element_type=F32)
            rows[k, p * ROWS : (p + 1) * ROWS, :] = spread.astype(BF)
        return carry

    lax.fori_loop(0, K, spread_step, 0, unroll=27)
    on_weights("wait", core, rep, *weights)

    def step(k, carry):
        product = lax.dot_general(
            rows[k], full[k], (((1,), (1,)), ((), ())), preferred_element_type=F32
        )
        for p in range(PAIRS):
            acc[ins[0, p, k]] += product[p * ROWS : (p + 1) * ROWS]
        return carry

    lax.fori_loop(0, K, step, 0, unroll=27)
    local[...] = acc[0:8]
    face_x[0:4] = acc[pl.ds(8 + 4 * (1 - core), 4)].astype(BF)
    face_x[4:6] = jnp.zeros((2, ROWS, C), BF)
    even = ends()[1]
    first[0:4] = acc[pl.ds(16 + 4 * even, 4)].astype(BF)
    first[4] = acc[24 + 2 * (1 - core) + even].astype(BF)
    second[0:4] = acc[pl.ds(20 - 4 * even, 4)].astype(BF)
    second[4] = acc[25 + 2 * (1 - core) - even].astype(BF)


def input_kernel(face, corner, local, from_x, first, second, out, acc):
    i, even = ends()
    acc[...] = local[...]
    for n in range(4):
        acc[face[0, 1 - i, n]] += from_x[n].astype(F32)
        acc[face[0, 2 + even, n]] += first[n].astype(F32)
        acc[face[0, 3 - even, n]] += second[n].astype(F32)
    acc[corner[0, 0, 2 * (1 - i) + even]] += from_x[4].astype(F32)
    acc[corner[0, 0, 2 * (1 - i) + 1 - even]] += from_x[5].astype(F32)
    out[...] = acc[...].astype(BF)


def plane_kernel(spread, out):
    for k in range(K):
        total = spread[0, k].astype(F32)
        for n in range(1, 16):
            total = total + spread[n, k].astype(F32)
        out[k // 4, k % 4] = total.astype(BF)
    for k in range(K, KPAD):
        out[k // 4, k % 4] = jnp.zeros((16, 128), BF)


def depth_kernel(spread, out):
    for k in range(4):
        total = spread[0, k].astype(F32)
        for n in range(1, 8):
            total = total + spread[n, k].astype(F32)
        for n in range(16):
            out[n, k] = total.astype(BF)


def final_kernel(scale, *refs):
    core, _, _, y_at, _ = places()
    out = refs[8]
    first = pl.program_id(0) * 9

    def run(turn):
        def step(n, carry):
            k = first + n
            sides = []
            for side in range(2):
                halves = []
                for x in range(2):
                    pieces = [refs[side * 4 + (turn - y) % 4][x, k].astype(F32) for y in range(4)]
                    halves.append(jnp.concatenate(pieces, 0))
                sides.append(jnp.concatenate(halves, 1) * scale)
            low = jnp.where(core == 0, sides[0], sides[1])
            high = jnp.where(core == 0, sides[1], sides[0])
            out[n] = jnp.concatenate([low, high], 0).T
            return carry

        lax.fori_loop(0, 9, step, 0, unroll=3)

    for turn in range(4):
        pl.when(y_at == turn)(functools.partial(run, turn))


def members(key):
    found = {}
    for y in range(4):
        for rep in range(2):
            for half in range(2):
                for z in range(8):
                    for core in range(2):
                        x = half * 2 + rep
                        found.setdefault(key(core, x, y, z), []).append(flat_id(core, x, y, z))
    return list(found.values())


def exchange(value, key):
    return lax.all_to_all(
        value, ALL, split_axis=0, concat_axis=0, axis_index_groups=members(key), tiled=False
    )


def body(feats, weight, cotan, face_send, corner_send, pair_out, pair_in, row_map):
    blocks = feats.reshape(NB, ROWS, C)
    lists = [("s", face_send), ("s", corner_send.swapaxes(1, 2))]
    pairs = [("s", v.swapaxes(1, 2)) for v in (pair_out, pair_in)] + [("v", row_map[0])]
    five, six = shape_of(5, ROWS, C), shape_of(6, ROWS, C)

    face_x, first, second = call(pick_kernel, lists + [("v", blocks)], [six, five, five])
    from_x = shift(face_x, core=1)
    first = swap_y(lax.dynamic_update_slice(first, from_x[4:5], (4, 0, 0)), 0)
    second = swap_y(lax.dynamic_update_slice(second, from_x[5:6], (4, 0, 0)), 1)
    part = lax.dynamic_slice_in_dim(weight, lax.axis_index("gx") * 128, 128, 1)
    far = lax.ppermute(
        tie(part, from_x), ALL, torus_perm(lambda c, x, y, z: (c, x + (1 if c == 0 else -1), y, z))
    )
    far = tie(far, first, second)
    far_other = shift(far, core=1)

    rows = call(
        gather_kernel,
        pairs[1:] + [("a", v) for v in (blocks, from_x, first, second)],
        [shape_of(K, PAIRS * ROWS, C)],
        [pltpu.VMEM((EXT, ROWS, C), BF), pltpu.SemaphoreType.DMA((6,))],
        pl.CostEstimate(flops=2_000_000_000, bytes_accessed=9_000_000, transcendentals=0),
    )[0]
    act, grad, keep, send = call(
        forward_kernel,
        pairs[:1]
        + [("v", rows)]
        + [("a", v) for v in (weight, far, far_other)]
        + [("h", cotan.reshape(NB, ROWS, C))],
        [
            shape_of(NB, ROWS, C),
            shape_of(NB, ROWS, C),
            shape_of(16, K, 16, 128),
            shape_of(16, K, 16, 128),
        ],
        [
            pltpu.VMEM((K, C, C), BF),
            pltpu.VMEM((NB, ROWS, C), F32),
            pltpu.VMEM((NB, C, ROWS), BF),
            pltpu.VMEM((NB, ROWS, C), BF),
            pltpu.SemaphoreType.DMA((4,)),
        ],
        pl.CostEstimate(flops=5_000_000_000, bytes_accessed=12_000_000, transcendentals=0),
    )
    got = shift(send, core=1)
    local, back_x, to_first, to_second = call(
        backward_kernel,
        pairs
        + [("v", grad)]
        + [("a", v) for v in (weight, far, far_other)],
        [shape_of(NB, ROWS, C, dtype=F32), six, five, five],
        [
            pltpu.VMEM((K, C, C), BF),
            pltpu.VMEM((K, PAIRS * ROWS, C), BF),
            pltpu.VMEM((EXT, ROWS, C), F32),
            pltpu.SemaphoreType.DMA((3,)),
        ],
        pl.CostEstimate(flops=5_000_000_000, bytes_accessed=10_000_000, transcendentals=0),
    )
    paired = (tie(keep, to_first).astype(F32) + got.astype(F32)).astype(BF)
    spread = exchange(paired, lambda c, x, y, z: (c, z))
    first = swap_y(tie(to_first, spread), 0)
    second = swap_y(tie(to_second, spread), 1)
    plane = call(plane_kernel, [("v", spread)], [shape_of(8, 4, 16, 128)])[0]
    spread = exchange(plane, lambda c, x, y, z: (c, x, y))
    depth = call(depth_kernel, [("v", spread)], [shape_of(16, 4, 16, 128)])[0]
    all_x = exchange(depth, lambda c, x, y, z: (c, x % 2, y))
    all_x = all_x.reshape(2, KPAD, 16, 128)[:, :K]
    back_x = lax.dynamic_update_slice(back_x, first[4:5], (4, 0, 0))
    back_x = lax.dynamic_update_slice(back_x, second[4:5], (5, 0, 0))
    return_x = shift(back_x, core=1)
    mine = [all_x] + [shift(all_x, y=s) for s in range(1, 4)]
    other = [shift(tie(piece, first, second), core=1) for piece in mine]

    input_grad = call(
        input_kernel,
        lists + [("v", v) for v in (local, return_x, first, second)],
        [shape_of(NB, ROWS, C)],
        [pltpu.VMEM((NB, ROWS, C), F32)],
    )[0]
    tiles = lax.axis_size("gx") * lax.axis_size("gy") * lax.axis_size("rep")
    scale = float((tiles * PAIRS * ROWS) ** (-0.5))
    pieces = mine + other
    weight_grad = pl.pallas_call(
        functools.partial(final_kernel, scale),
        grid=(3,),
        out_shape=shape_of(K, C, 128, dtype=F32),
        in_specs=[pl.BlockSpec((2, K, 16, 128), lambda n: (0, 0, 0, 0))] * 8,
        out_specs=pl.BlockSpec((9, C, 128), lambda n: (n, 0, 0)),
        compiler_params=PARAMS,
    )(*pieces)
    return act.reshape(-1, C), input_grad.reshape(-1, C), weight_grad


def solution(mesh):
    tiles = ("gx", "gy", "rep")
    in_specs = (
        P(tiles, None),
        P(None, None, "rep"),
        P(tiles, None),
        P(tiles, None, None),
        P(tiles, None, None),
        P(tiles, None, None),
        P(tiles, None, None),
        P(tiles, None, None, None),
    )
    out_specs = (P(tiles, None), P(tiles, None), P(None, None, "rep"))
    return jax.shard_map(body, mesh=mesh, in_specs=in_specs, out_specs=out_specs, check_vma=False)
```

```python
import functools

import jax
import jax.numpy as jnp
from jax import lax
from jax.experimental import pallas as pl
from jax.experimental.pallas import tpu as pltpu
from jax.sharding import PartitionSpec as P

ALL = ("gx", "gy", "rep")
K, C, NB, ROWS, PAIRS = 27, 256, 8, 128, 4
EXT = 29
KPAD = 32
BF, F32 = jnp.bfloat16, jnp.float32
VM = pl.BlockSpec(memory_space=pltpu.VMEM)
SM = pl.BlockSpec(memory_space=pltpu.SMEM)
PARAMS = pltpu.CompilerParams(vmem_limit_bytes=26 * 1024 * 1024)


def shape_of(*dims, dtype=BF):
    return jax.ShapeDtypeStruct(dims, dtype)


def call(kernel, ins, outs, scratch=(), cost=None):
    place = {
        "s": SM,
        "v": VM,
        "a": pl.BlockSpec(memory_space=pl.ANY),
        "h": pl.BlockSpec(memory_space=pltpu.HBM),
    }
    outs = [out if isinstance(out, tuple) else ("v", out) for out in outs]
    return pl.pallas_call(
        kernel,
        out_shape=[out for _, out in outs],
        in_specs=[place[kind] for kind, _ in ins],
        out_specs=[place[kind] for kind, _ in outs],
        scratch_shapes=list(scratch),
        compiler_params=PARAMS,
        cost_estimate=cost,
    )(*[value for _, value in ins])


def tie(value, *after):
    return lax.optimization_barrier((value, *after))[0]


def places():
    gy = lax.axis_index("gy")
    return lax.axis_index("gx"), lax.axis_index("rep"), gy % 2, gy // 2 % 4, gy // 8


def flat_id(core, x, y, z):
    return (core * 64 + ((z % 8) * 4 + y % 4) * 2 + (x % 4) // 2) * 2 + x % 2


def torus_perm(move):
    pairs = []
    for core in range(2):
        for z in range(8):
            for y in range(4):
                for x in range(4):
                    pairs.append((flat_id(core, x, y, z), flat_id(*move(core, x, y, z))))
    return pairs


def shift(value, **by):
    def move(core, x, y, z):
        return (
            (core + by.get("core", 0)) % 2,
            x + by.get("x", 0),
            y + by.get("y", 0),
            z + by.get("z", 0),
        )

    return lax.ppermute(value, ALL, torus_perm(move))


def swap_y(value, which):
    pairs = []
    for j in range(64):
        to = (j ^ 1) if which == 0 else (j + 1 if j % 2 else j - 1)
        if 0 <= to < 64:
            pairs += [((i * 64 + j) * 2 + r, (i * 64 + to) * 2 + r) for i in (0, 1) for r in (0, 1)]
    return lax.ppermute(value, ALL, pairs)


def ends():
    return lax.axis_index("gx"), 1 - lax.axis_index("gy") % 2


def pick_kernel(face, corner, feats, face_x, first, second):
    i, even = ends()
    for n in range(4):
        face_x[n] = feats[face[0, 1 - i, n]]
        first[n] = feats[face[0, 2 + even, n]]
        second[n] = feats[face[0, 3 - even, n]]
    face_x[4] = feats[corner[0, 0, 2 * (1 - i) + even]]
    face_x[5] = feats[corner[0, 0, 2 * (1 - i) + 1 - even]]
    first[4] = face_x[4]
    second[4] = face_x[5]


def weight_of(k, core, rep, y_at, own, near, other):
    ours = [near[(y_at - y) & 3, k] for y in range(4)]
    theirs = [other[(y_at - y) & 3, k] for y in range(4)]
    ours, theirs = jnp.concatenate(ours, 0), jnp.concatenate(theirs, 0)
    first, second = jnp.where(core == 0, ours, theirs), jnp.where(core == 0, theirs, ours)
    mine, far = own[k], jnp.concatenate([first, second], 0)
    low, high = jnp.where(rep == 0, mine, far), jnp.where(rep == 0, far, mine)
    return jnp.concatenate([low, high], 1)


def gather_kernel(ins, maps, feats, from_x, first, second, rows, ext, sems):
    core, even = ends()
    ext[8:16] = jnp.zeros((8, ROWS, C), BF)
    ext[24:29] = jnp.zeros((5, ROWS, C), BF)
    corners = 24 + 2 * (1 - core)
    copies = [
        pltpu.make_async_copy(feats, ext.at[0:8], sems.at[0]),
        pltpu.make_async_copy(from_x.at[0:4], ext.at[pl.ds(8 + 4 * (1 - core), 4)], sems.at[1]),
        pltpu.make_async_copy(first.at[0:4], ext.at[pl.ds(16 + 4 * even, 4)], sems.at[2]),
        pltpu.make_async_copy(second.at[0:4], ext.at[pl.ds(20 - 4 * even, 4)], sems.at[3]),
        pltpu.make_async_copy(first.at[4], ext.at[corners + even], sems.at[4]),
        pltpu.make_async_copy(second.at[4], ext.at[corners + 1 - even], sems.at[5]),
    ]
    for copy in copies:
        copy.start()
    lanes = lax.broadcasted_iota(jnp.int32, (ROWS, ROWS), 0)
    for copy in copies:
        copy.wait()

    def step(k, carry):
        map_k = maps[k]
        for p in range(PAIRS):
            hot = (lanes == map_k[p : p + 1, :]).astype(F32).astype(BF)
            picked = lax.dot_general(
                hot, ext[ins[0, p, k]], (((0,), (0,)), ((), ())), preferred_element_type=F32
            )
            rows[k, p * ROWS : (p + 1) * ROWS, :] = picked.astype(BF)
        return carry

    lax.fori_loop(0, K, step, 0, unroll=27)


def forward_kernel(
    outs, rows, own, near, other, cotan_in,
    act, grad, keep, send,
    acc, flipped, cotan, sem,
):
    core, rep, _, y_at, _ = places()
    cotan_copy = pltpu.make_async_copy(cotan_in, cotan, sem)
    cotan_copy.start()
    acc[...] = jnp.zeros_like(acc)

    def product_step(k, carry):
        full = weight_of(k, core, rep, y_at, own, near, other)
        product = jnp.dot(rows[k], full, preferred_element_type=F32)
        for p in range(PAIRS):
            acc[outs[0, p, k]] += product[p * ROWS : (p + 1) * ROWS]
        return carry

    lax.fori_loop(0, K, product_step, 0, unroll=27)

    cotan_copy.wait()

    def grad_step(b, carry):
        value = acc[b]
        sigma = 1.0 / (1.0 + jnp.exp(-value))
        act[b] = (value * sigma).astype(BF)
        up = cotan[b].astype(F32) * (sigma * (1.0 + value * (1.0 - sigma)))
        grad[b] = up.astype(BF)
        flipped[b] = up.T.astype(BF)
        return carry

    lax.fori_loop(0, NB, grad_step, 0, unroll=4)

    def weight_step(k, carry):
        left = jnp.concatenate([flipped[outs[0, p, k]] for p in range(PAIRS)], axis=1)
        part = jnp.dot(left, rows[k], preferred_element_type=F32)
        for side in range(2):
            first = part[side * 128 : side * 128 + 64]
            second = part[side * 128 + 64 : side * 128 + 128]
            kept = jnp.where(core == 0, first, second).astype(BF)
            sent = jnp.where(core == 0, second, first).astype(BF)
            for y in range(4):
                for x in range(2):
                    at = (slice(y * 16, y * 16 + 16), slice(x * 128, x * 128 + 128))
                    keep[y * 4 + side * 2 + x, k] = kept[at]
                    send[y * 4 + side * 2 + x, k] = sent[at]
        return carry

    lax.fori_loop(0, K, weight_step, 0, unroll=27)


def backward_kernel(
    outs, ins, maps, grad, own, near, other,
    local, face_x, first, second,
    rows, acc,
):
    core, rep, _, y_at, _ = places()
    acc[...] = jnp.zeros_like(acc)
    lanes = lax.broadcasted_iota(jnp.int32, (ROWS, ROWS), 0)

    def spread_step(k, carry):
        map_k = maps[k]
        for p in range(PAIRS):
            hot = (lanes == map_k[p : p + 1, :]).astype(F32).astype(BF)
            spread = jnp.dot(hot, grad[outs[0, p, k]], preferred_element_type=F32)
            rows[k, p * ROWS : (p + 1) * ROWS, :] = spread.astype(BF)
        return carry

    lax.fori_loop(0, K, spread_step, 0, unroll=27)

    def step(k, carry):
        full = weight_of(k, core, rep, y_at, own, near, other)
        product = lax.dot_general(
            rows[k], full, (((1,), (1,)), ((), ())), preferred_element_type=F32
        )
        for p in range(PAIRS):
            acc[ins[0, p, k]] += product[p * ROWS : (p + 1) * ROWS]
        return carry

    lax.fori_loop(0, K, step, 0, unroll=27)
    local[...] = acc[0:8]
    face_x[0:4] = acc[pl.ds(8 + 4 * (1 - core), 4)].astype(BF)
    face_x[4:6] = jnp.zeros((2, ROWS, C), BF)
    even = ends()[1]
    first[0:4] = acc[pl.ds(16 + 4 * even, 4)].astype(BF)
    first[4] = acc[24 + 2 * (1 - core) + even].astype(BF)
    second[0:4] = acc[pl.ds(20 - 4 * even, 4)].astype(BF)
    second[4] = acc[25 + 2 * (1 - core) - even].astype(BF)


def input_kernel(face, corner, local, from_x, first, second, out, acc):
    i, even = ends()
    acc[...] = local[...]
    for n in range(4):
        acc[face[0, 1 - i, n]] += from_x[n].astype(F32)
        acc[face[0, 2 + even, n]] += first[n].astype(F32)
        acc[face[0, 3 - even, n]] += second[n].astype(F32)
    acc[corner[0, 0, 2 * (1 - i) + even]] += from_x[4].astype(F32)
    acc[corner[0, 0, 2 * (1 - i) + 1 - even]] += from_x[5].astype(F32)
    out[...] = acc[...].astype(BF)


def plane_kernel(spread, out):
    for k in range(K):
        total = spread[0, k].astype(F32)
        for n in range(1, 16):
            total = total + spread[n, k].astype(F32)
        out[k // 4, k % 4] = total.astype(BF)
    for k in range(K, KPAD):
        out[k // 4, k % 4] = jnp.zeros((16, 128), BF)


def depth_kernel(spread, out):
    for k in range(4):
        total = spread[0, k].astype(F32)
        for n in range(1, 8):
            total = total + spread[n, k].astype(F32)
        for n in range(16):
            out[n, k] = total.astype(BF)


def final_kernel(scale, *refs):
    core, _, _, y_at, _ = places()
    out = refs[8]
    first = pl.program_id(0) * 9

    def run(turn):
        def step(n, carry):
            k = first + n
            sides = []
            for side in range(2):
                halves = []
                for x in range(2):
                    pieces = [refs[side * 4 + (turn - y) % 4][x, k] for y in range(4)]
                    halves.append(jnp.concatenate(pieces, 0))
                sides.append(jnp.concatenate(halves, 1))
            low = jnp.where(core == 0, sides[0], sides[1])
            high = jnp.where(core == 0, sides[1], sides[0])
            out[n] = jnp.concatenate([low, high], 0).T.astype(F32) * scale
            return carry

        lax.fori_loop(0, 9, step, 0, unroll=3)

    for turn in range(4):
        pl.when(y_at == turn)(functools.partial(run, turn))


def members(key):
    found = {}
    for y in range(4):
        for rep in range(2):
            for half in range(2):
                for z in range(8):
                    for core in range(2):
                        x = half * 2 + rep
                        found.setdefault(key(core, x, y, z), []).append(flat_id(core, x, y, z))
    return list(found.values())


def exchange(value, key):
    return lax.all_to_all(
        value, ALL, split_axis=0, concat_axis=0, axis_index_groups=members(key), tiled=False
    )


def body(feats, weight, cotan, face_send, corner_send, pair_out, pair_in, row_map):
    blocks = feats.reshape(NB, ROWS, C)
    lists = [("s", face_send), ("s", corner_send.swapaxes(1, 2))]
    pairs = [("s", v.swapaxes(1, 2)) for v in (pair_out, pair_in)] + [("v", row_map[0])]
    five, six = shape_of(5, ROWS, C), shape_of(6, ROWS, C)

    face_x, first, second = call(pick_kernel, lists + [("v", blocks)], [six, five, five])
    from_x = shift(face_x, core=1)
    first = swap_y(lax.dynamic_update_slice(first, from_x[4:5], (4, 0, 0)), 0)
    second = swap_y(lax.dynamic_update_slice(second, from_x[5:6], (4, 0, 0)), 1)
    row = lax.axis_index("gx") * 128 + places()[3] * 32
    part = lax.dynamic_slice_in_dim(weight, row, 32, 1)
    far = lax.ppermute(
        part, ALL, torus_perm(lambda c, x, y, z: (c, x + (1 if c == 0 else -1), y, z))
    )
    near = jnp.stack([far] + [tie(shift(far, y=s), first, second) for s in range(1, 4)], 0)
    other = shift(near, core=1)

    rows = call(
        gather_kernel,
        pairs[1:] + [("a", v) for v in (blocks, from_x, first, second)],
        [shape_of(K, PAIRS * ROWS, C)],
        [pltpu.VMEM((EXT, ROWS, C), BF), pltpu.SemaphoreType.DMA((6,))],
        pl.CostEstimate(flops=2_000_000_000, bytes_accessed=9_000_000, transcendentals=0),
    )[0]
    act, grad, keep, send = call(
        forward_kernel,
        pairs[:1]
        + [("v", rows)]
        + [("v", v) for v in (weight, near, other)]
        + [("h", cotan.reshape(NB, ROWS, C))],
        [
            shape_of(NB, ROWS, C),
            shape_of(NB, ROWS, C),
            shape_of(16, K, 16, 128),
            shape_of(16, K, 16, 128),
        ],
        [
            pltpu.VMEM((NB, ROWS, C), F32),
            pltpu.VMEM((NB, C, ROWS), BF),
            pltpu.VMEM((NB, ROWS, C), BF),
            pltpu.SemaphoreType.DMA,
        ],
        pl.CostEstimate(flops=5_000_000_000, bytes_accessed=12_000_000, transcendentals=0),
    )
    got = shift(send, core=1)
    local, back_x, to_first, to_second = call(
        backward_kernel,
        pairs
        + [("v", grad)]
        + [("v", v) for v in (weight, near, other)],
        [shape_of(NB, ROWS, C, dtype=F32), six, five, five],
        [
            pltpu.VMEM((K, PAIRS * ROWS, C), BF),
            pltpu.VMEM((EXT, ROWS, C), F32),
        ],
        pl.CostEstimate(flops=5_000_000_000, bytes_accessed=10_000_000, transcendentals=0),
    )
    paired = (tie(keep, to_first).astype(F32) + got.astype(F32)).astype(BF)
    spread = exchange(paired, lambda c, x, y, z: (c, z))
    first = swap_y(tie(to_first, spread), 0)
    second = swap_y(tie(to_second, spread), 1)
    plane = call(plane_kernel, [("v", spread)], [shape_of(8, 4, 16, 128)])[0]
    spread = exchange(plane, lambda c, x, y, z: (c, x, y))
    depth = call(depth_kernel, [("v", spread)], [shape_of(16, 4, 16, 128)])[0]
    all_x = exchange(depth, lambda c, x, y, z: (c, x % 2, y))
    all_x = all_x.reshape(2, KPAD, 16, 128)[:, :K]
    back_x = lax.dynamic_update_slice(back_x, first[4:5], (4, 0, 0))
    back_x = lax.dynamic_update_slice(back_x, second[4:5], (5, 0, 0))
    return_x = shift(back_x, core=1)
    mine = [all_x] + [shift(all_x, y=s) for s in range(1, 4)]
    input_grad = call(
        input_kernel,
        lists + [("v", v) for v in (local, return_x, first, second)],
        [shape_of(NB, ROWS, C)],
        [pltpu.VMEM((NB, ROWS, C), F32)],
    )[0]
    other = [shift(piece, core=1) for piece in mine[:3]]
    other.append(shift(tie(mine[3], input_grad), core=1))
    tiles = lax.axis_size("gx") * lax.axis_size("gy") * lax.axis_size("rep")
    scale = float((tiles * PAIRS * ROWS) ** (-0.5))
    pieces = mine + other
    weight_grad = pl.pallas_call(
        functools.partial(final_kernel, scale),
        grid=(3,),
        out_shape=shape_of(K, C, 128, dtype=F32),
        in_specs=[pl.BlockSpec((2, K, 16, 128), lambda n: (0, 0, 0, 0))] * 8,
        out_specs=pl.BlockSpec((9, C, 128), lambda n: (n, 0, 0)),
        compiler_params=PARAMS,
    )(*pieces)
    return act.reshape(-1, C), input_grad.reshape(-1, C), weight_grad


def solution(mesh):
    tiles = ("gx", "gy", "rep")
    in_specs = (
        P(tiles, None),
        P(None, None, "rep"),
        P(tiles, None),
        P(tiles, None, None),
        P(tiles, None, None),
        P(tiles, None, None),
        P(tiles, None, None),
        P(tiles, None, None, None),
    )
    out_specs = (P(tiles, None), P(tiles, None), P(None, None, "rep"))
    return jax.shard_map(body, mesh=mesh, in_specs=in_specs, out_specs=out_specs, check_vma=False)
```

```python
import functools

import jax
import jax.numpy as jnp
from jax import lax
from jax.experimental import pallas as pl
from jax.experimental.pallas import tpu as pltpu
from jax.sharding import PartitionSpec as P

ALL = ("gx", "gy", "rep")
K, C, NB, ROWS, PAIRS = 27, 256, 8, 128, 4
EXT = 29
KPAD = 32
BF, F32 = jnp.bfloat16, jnp.float32
VM = pl.BlockSpec(memory_space=pltpu.VMEM)
SM = pl.BlockSpec(memory_space=pltpu.SMEM)
PARAMS = pltpu.CompilerParams(vmem_limit_bytes=26 * 1024 * 1024)


def shape_of(*dims, dtype=BF):
    return jax.ShapeDtypeStruct(dims, dtype)


def call(kernel, ins, outs, scratch=(), cost=None):
    place = {
        "s": SM,
        "v": VM,
        "a": pl.BlockSpec(memory_space=pl.ANY),
        "h": pl.BlockSpec(memory_space=pltpu.HBM),
    }
    outs = [out if isinstance(out, tuple) else ("v", out) for out in outs]
    return pl.pallas_call(
        kernel,
        out_shape=[out for _, out in outs],
        in_specs=[place[kind] for kind, _ in ins],
        out_specs=[place[kind] for kind, _ in outs],
        scratch_shapes=list(scratch),
        compiler_params=PARAMS,
        cost_estimate=cost,
    )(*[value for _, value in ins])


def tie(value, *after):
    return lax.optimization_barrier((value, *after))[0]


def places():
    gy = lax.axis_index("gy")
    return lax.axis_index("gx"), lax.axis_index("rep"), gy % 2, gy // 2 % 4, gy // 8


def flat_id(core, x, y, z):
    return (core * 64 + ((z % 8) * 4 + y % 4) * 2 + (x % 4) // 2) * 2 + x % 2


def torus_perm(move):
    pairs = []
    for core in range(2):
        for z in range(8):
            for y in range(4):
                for x in range(4):
                    pairs.append((flat_id(core, x, y, z), flat_id(*move(core, x, y, z))))
    return pairs


def shift(value, **by):
    def move(core, x, y, z):
        return (
            (core + by.get("core", 0)) % 2,
            x + by.get("x", 0),
            y + by.get("y", 0),
            z + by.get("z", 0),
        )

    return lax.ppermute(value, ALL, torus_perm(move))


def swap_y(value, which):
    pairs = []
    for j in range(64):
        to = (j ^ 1) if which == 0 else (j + 1 if j % 2 else j - 1)
        if 0 <= to < 64:
            pairs += [((i * 64 + j) * 2 + r, (i * 64 + to) * 2 + r) for i in (0, 1) for r in (0, 1)]
    return lax.ppermute(value, ALL, pairs)


def ends():
    return lax.axis_index("gx"), 1 - lax.axis_index("gy") % 2


def pick_kernel(face, corner, feats, face_x, first, second):
    i, even = ends()
    for n in range(4):
        face_x[n] = feats[face[0, 1 - i, n]]
        first[n] = feats[face[0, 2 + even, n]]
        second[n] = feats[face[0, 3 - even, n]]
    face_x[4] = feats[corner[0, 0, 2 * (1 - i) + even]]
    face_x[5] = feats[corner[0, 0, 2 * (1 - i) + 1 - even]]
    first[4] = face_x[4]
    second[4] = face_x[5]


def weight_of(k, core, rep, y_at, own, near, other):
    ours = [near[(y_at - y) & 3, k] for y in range(4)]
    theirs = [other[(y_at - y) & 3, k] for y in range(4)]
    ours, theirs = jnp.concatenate(ours, 0), jnp.concatenate(theirs, 0)
    first, second = jnp.where(core == 0, ours, theirs), jnp.where(core == 0, theirs, ours)
    mine, far = own[k], jnp.concatenate([first, second], 0)
    low, high = jnp.where(rep == 0, mine, far), jnp.where(rep == 0, far, mine)
    return jnp.concatenate([low, high], 1)


def gather_kernel(ins, maps, feats, from_x, first, second, rows, ext, sems):
    core, even = ends()
    ext[8:16] = jnp.zeros((8, ROWS, C), BF)
    ext[24:29] = jnp.zeros((5, ROWS, C), BF)
    corners = 24 + 2 * (1 - core)
    copies = [
        pltpu.make_async_copy(feats, ext.at[0:8], sems.at[0]),
        pltpu.make_async_copy(from_x.at[0:4], ext.at[pl.ds(8 + 4 * (1 - core), 4)], sems.at[1]),
        pltpu.make_async_copy(first.at[0:4], ext.at[pl.ds(16 + 4 * even, 4)], sems.at[2]),
        pltpu.make_async_copy(second.at[0:4], ext.at[pl.ds(20 - 4 * even, 4)], sems.at[3]),
        pltpu.make_async_copy(first.at[4], ext.at[corners + even], sems.at[4]),
        pltpu.make_async_copy(second.at[4], ext.at[corners + 1 - even], sems.at[5]),
    ]
    for copy in copies:
        copy.start()
    lanes = lax.broadcasted_iota(jnp.int32, (ROWS, ROWS), 0)
    for copy in copies:
        copy.wait()

    def step(k, carry):
        map_k = maps[k]
        for p in range(PAIRS):
            hot = (lanes == map_k[p : p + 1, :]).astype(F32).astype(BF)
            picked = lax.dot_general(
                hot, ext[ins[0, p, k]], (((0,), (0,)), ((), ())), preferred_element_type=F32
            )
            rows[k, p * ROWS : (p + 1) * ROWS, :] = picked.astype(BF)
        return carry

    lax.fori_loop(0, K, step, 0, unroll=27)


def forward_kernel(
    outs, rows, own, near, other, cotan_in,
    act, grad, keep, send,
    acc, flipped, cotan, sem,
):
    core, rep, _, y_at, _ = places()
    cotan_copy = pltpu.make_async_copy(cotan_in, cotan, sem)
    cotan_copy.start()
    acc[...] = jnp.zeros_like(acc)

    def product_step(k, carry):
        full = weight_of(k, core, rep, y_at, own, near, other)
        product = jnp.dot(rows[k], full, preferred_element_type=F32)
        for p in range(PAIRS):
            acc[outs[0, p, k]] += product[p * ROWS : (p + 1) * ROWS]
        return carry

    lax.fori_loop(0, K, product_step, 0, unroll=27)

    cotan_copy.wait()

    def grad_step(b, carry):
        value = acc[b]
        sigma = 1.0 / (1.0 + jnp.exp(-value))
        act[b] = (value * sigma).astype(BF)
        up = cotan[b].astype(F32) * (sigma * (1.0 + value * (1.0 - sigma)))
        grad[b] = up.astype(BF)
        flipped[b] = up.T.astype(BF)
        return carry

    lax.fori_loop(0, NB, grad_step, 0, unroll=4)

    def weight_step(k, carry):
        left = jnp.concatenate([flipped[outs[0, p, k]] for p in range(PAIRS)], axis=1)
        part = jnp.dot(left, rows[k], preferred_element_type=F32)
        for side in range(2):
            first = part[side * 128 : side * 128 + 64]
            second = part[side * 128 + 64 : side * 128 + 128]
            kept = jnp.where(core == 0, first, second).astype(BF)
            sent = jnp.where(core == 0, second, first).astype(BF)
            for y in range(4):
                for x in range(2):
                    at = (slice(y * 16, y * 16 + 16), slice(x * 128, x * 128 + 128))
                    keep[y * 4 + side * 2 + x, k] = kept[at]
                    send[y * 4 + side * 2 + x, k] = sent[at]
        return carry

    lax.fori_loop(0, K, weight_step, 0, unroll=27)


def backward_kernel(
    outs, ins, maps, grad, own, near, other,
    local, face_x, first, second,
    rows, acc,
):
    core, rep, _, y_at, _ = places()
    acc[...] = jnp.zeros_like(acc)
    lanes = lax.broadcasted_iota(jnp.int32, (ROWS, ROWS), 0)

    def spread_step(k, carry):
        map_k = maps[k]
        for p in range(PAIRS):
            hot = (lanes == map_k[p : p + 1, :]).astype(F32).astype(BF)
            spread = jnp.dot(hot, grad[outs[0, p, k]], preferred_element_type=F32)
            rows[k, p * ROWS : (p + 1) * ROWS, :] = spread.astype(BF)
        return carry

    lax.fori_loop(0, K, spread_step, 0, unroll=27)

    def step(k, carry):
        full = weight_of(k, core, rep, y_at, own, near, other)
        product = lax.dot_general(
            rows[k], full, (((1,), (1,)), ((), ())), preferred_element_type=F32
        )
        for p in range(PAIRS):
            acc[ins[0, p, k]] += product[p * ROWS : (p + 1) * ROWS]
        return carry

    lax.fori_loop(0, K, step, 0, unroll=27)
    local[...] = acc[0:8]
    face_x[0:4] = acc[pl.ds(8 + 4 * (1 - core), 4)].astype(BF)
    face_x[4:6] = jnp.zeros((2, ROWS, C), BF)
    even = ends()[1]
    first[0:4] = acc[pl.ds(16 + 4 * even, 4)].astype(BF)
    first[4] = acc[24 + 2 * (1 - core) + even].astype(BF)
    second[0:4] = acc[pl.ds(20 - 4 * even, 4)].astype(BF)
    second[4] = acc[25 + 2 * (1 - core) - even].astype(BF)


def input_kernel(face, corner, local, from_x, first, second, out, acc):
    i, even = ends()
    acc[...] = local[...]
    for n in range(4):
        acc[face[0, 1 - i, n]] += from_x[n].astype(F32)
        acc[face[0, 2 + even, n]] += first[n].astype(F32)
        acc[face[0, 3 - even, n]] += second[n].astype(F32)
    acc[corner[0, 0, 2 * (1 - i) + even]] += from_x[4].astype(F32)
    acc[corner[0, 0, 2 * (1 - i) + 1 - even]] += from_x[5].astype(F32)
    out[...] = acc[...].astype(BF)


def plane_kernel(spread, out):
    for k in range(K):
        total = spread[0, k].astype(F32)
        for n in range(1, 16):
            total = total + spread[n, k].astype(F32)
        out[k // 4, k % 4] = total.astype(BF)
    for k in range(K, KPAD):
        out[k // 4, k % 4] = jnp.zeros((16, 128), BF)


def depth_kernel(spread, out):
    for k in range(4):
        total = spread[0, k].astype(F32)
        for n in range(1, 8):
            total = total + spread[n, k].astype(F32)
        for n in range(16):
            out[n, k] = total.astype(BF)


def final_kernel(scale, *refs):
    core, _, _, y_at, _ = places()
    out = refs[8]
    first = pl.program_id(0) * 9

    def run(turn):
        def step(n, carry):
            k = first + n
            sides = []
            for side in range(2):
                halves = []
                for x in range(2):
                    pieces = [refs[side * 4 + (turn - y) % 4][x, k] for y in range(4)]
                    halves.append(jnp.concatenate(pieces, 0))
                sides.append(jnp.concatenate(halves, 1))
            low = jnp.where(core == 0, sides[0], sides[1])
            high = jnp.where(core == 0, sides[1], sides[0])
            out[n] = jnp.concatenate([low, high], 0).T.astype(F32) * scale
            return carry

        lax.fori_loop(0, 9, step, 0, unroll=3)

    for turn in range(4):
        pl.when(y_at == turn)(functools.partial(run, turn))


def members(key):
    found = {}
    for y in range(4):
        for rep in range(2):
            for half in range(2):
                for z in range(8):
                    for core in range(2):
                        x = half * 2 + rep
                        found.setdefault(key(core, x, y, z), []).append(flat_id(core, x, y, z))
    return list(found.values())


def exchange(value, key):
    return lax.all_to_all(
        value, ALL, split_axis=0, concat_axis=0, axis_index_groups=members(key), tiled=False
    )


def body(feats, weight, cotan, face_send, corner_send, pair_out, pair_in, row_map):
    blocks = feats.reshape(NB, ROWS, C)
    lists = [("s", face_send), ("s", corner_send.swapaxes(1, 2))]
    pairs = [("s", v.swapaxes(1, 2)) for v in (pair_out, pair_in)] + [("v", row_map[0])]
    five, six = shape_of(5, ROWS, C), shape_of(6, ROWS, C)

    face_x, first, second = call(pick_kernel, lists + [("v", blocks)], [six, five, five])
    from_x = shift(face_x, core=1)
    first = swap_y(lax.dynamic_update_slice(first, from_x[4:5], (4, 0, 0)), 0)
    second = swap_y(lax.dynamic_update_slice(second, from_x[5:6], (4, 0, 0)), 1)
    row = lax.axis_index("gx") * 128 + places()[3] * 32
    part = lax.dynamic_slice_in_dim(weight, row, 32, 1)
    far = lax.ppermute(
        part, ALL, torus_perm(lambda c, x, y, z: (c, x + (1 if c == 0 else -1), y, z))
    )
    near = jnp.stack([far] + [tie(shift(far, y=s), first, second) for s in range(1, 4)], 0)
    other = shift(near, core=1)

    rows = call(
        gather_kernel,
        pairs[1:] + [("a", v) for v in (blocks, from_x, first, second)],
        [shape_of(K, PAIRS * ROWS, C)],
        [pltpu.VMEM((EXT, ROWS, C), BF), pltpu.SemaphoreType.DMA((6,))],
        pl.CostEstimate(flops=2_000_000_000, bytes_accessed=9_000_000, transcendentals=0),
    )[0]
    act, grad, keep, send = call(
        forward_kernel,
        pairs[:1]
        + [("v", rows)]
        + [("v", v) for v in (weight, near, other)]
        + [("h", cotan.reshape(NB, ROWS, C))],
        [
            shape_of(NB, ROWS, C),
            shape_of(NB, ROWS, C),
            shape_of(16, K, 16, 128),
            shape_of(16, K, 16, 128),
        ],
        [
            pltpu.VMEM((NB, ROWS, C), F32),
            pltpu.VMEM((NB, C, ROWS), BF),
            pltpu.VMEM((NB, ROWS, C), BF),
            pltpu.SemaphoreType.DMA,
        ],
        pl.CostEstimate(flops=5_000_000_000, bytes_accessed=12_000_000, transcendentals=0),
    )
    got = shift(send, core=1)
    paired = (keep.astype(F32) + got.astype(F32)).astype(BF)
    local, back_x, to_first, to_second = call(
        backward_kernel,
        pairs
        + [("v", tie(grad, paired))]
        + [("v", v) for v in (weight, near, other)],
        [shape_of(NB, ROWS, C, dtype=F32), six, five, five],
        [
            pltpu.VMEM((K, PAIRS * ROWS, C), BF),
            pltpu.VMEM((EXT, ROWS, C), F32),
        ],
        pl.CostEstimate(flops=5_000_000_000, bytes_accessed=10_000_000, transcendentals=0),
    )
    spread = exchange(paired, lambda c, x, y, z: (c, z))
    first = swap_y(tie(to_first, spread), 0)
    second = swap_y(tie(to_second, spread), 1)
    plane = call(plane_kernel, [("v", spread)], [shape_of(8, 4, 16, 128)])[0]
    spread = exchange(plane, lambda c, x, y, z: (c, x, y))
    depth = call(depth_kernel, [("v", spread)], [shape_of(16, 4, 16, 128)])[0]
    all_x = exchange(depth, lambda c, x, y, z: (c, x % 2, y))
    all_x = all_x.reshape(2, KPAD, 16, 128)[:, :K]
    back_x = lax.dynamic_update_slice(back_x, first[4:5], (4, 0, 0))
    back_x = lax.dynamic_update_slice(back_x, second[4:5], (5, 0, 0))
    return_x = shift(back_x, core=1)
    mine = [all_x] + [shift(all_x, y=s) for s in range(1, 4)]
    input_grad = call(
        input_kernel,
        lists + [("v", v) for v in (local, return_x, first, second)],
        [shape_of(NB, ROWS, C)],
        [pltpu.VMEM((NB, ROWS, C), F32)],
    )[0]
    other = [shift(piece, core=1) for piece in mine[:3]]
    other.append(shift(tie(mine[3], input_grad), core=1))
    tiles = lax.axis_size("gx") * lax.axis_size("gy") * lax.axis_size("rep")
    scale = float((tiles * PAIRS * ROWS) ** (-0.5))
    pieces = mine + other
    weight_grad = pl.pallas_call(
        functools.partial(final_kernel, scale),
        grid=(3,),
        out_shape=shape_of(K, C, 128, dtype=F32),
        in_specs=[pl.BlockSpec((2, K, 16, 128), lambda n: (0, 0, 0, 0))] * 8,
        out_specs=pl.BlockSpec((9, C, 128), lambda n: (n, 0, 0)),
        compiler_params=PARAMS,
    )(*pieces)
    return act.reshape(-1, C), input_grad.reshape(-1, C), weight_grad


def solution(mesh):
    tiles = ("gx", "gy", "rep")
    in_specs = (
        P(tiles, None),
        P(None, None, "rep"),
        P(tiles, None),
        P(tiles, None, None),
        P(tiles, None, None),
        P(tiles, None, None),
        P(tiles, None, None),
        P(tiles, None, None, None),
    )
    out_specs = (P(tiles, None), P(tiles, None), P(None, None, "rep"))
    return jax.shard_map(body, mesh=mesh, in_specs=in_specs, out_specs=out_specs, check_vma=False)
```
